256 devices in a mesh: dp: 32 (over z_lo, x, core), ctx: 8 (over z_hi, y).
Axes of the slice: x: 4, y: 4, z: 8 (z_hi: 2, z_lo: 4; z = z_hi * 4 + z_lo), core: 2. Of those that a mesh axis runs over, the one named last changes fastest.
Arguments:
- queries: bfloat16 [32, 1024, 4096], P('dp', 'ctx'), may hold values from -4.5 to 4.5
- keys: bfloat16 [32, 1024, 1024], P('dp', 'ctx'), may hold values from -4 to 4
- values: bfloat16 [32, 1024, 1024], P('dp', 'ctx'), may hold values from -6 to 6
- prefix_keys: bfloat16 [128, 1024], replicated, may hold values from -6 to 6
- prefix_values: bfloat16 [128, 1024], replicated, may hold values from -6 to 6
- out_grad: bfloat16 [32, 1024, 4096], P('dp', 'ctx'), may hold values from -6 to 6
- boundaries: int32 [32, 8], P('dp'), may hold values from 0 to 448, as said below
- lengths: int32 [32], P('dp'), may hold values from 512 to 1024, as said below
- advantages: float32 [32, 8], P('dp'), may hold values from -4 to 4
Outputs:
- query_grad: bfloat16 [32, 1024, 4096], P('dp', 'ctx')
- key_grad: bfloat16 [32, 1024, 1024], P('dp', 'ctx')
- value_grad: bfloat16 [32, 1024, 1024], P('dp', 'ctx')
- prefix_key_grad: float32 [128, 1024], replicated
- prefix_value_grad: float32 [128, 1024], replicated
The draws below stay inside these ranges and needn't reach their ends.
Inputs may be any that keep to these rules, and one draw needn't show every extreme that they name: Each row begins at 0 and rises strictly; consecutive boundaries differ by at most 64. `lengths`: trajectory 0 always has length 1024.
All inputs are finite; a program needn't handle non-finite values.
Results may differ from the reference program's by a relative error of at most 0.019.
Values may be sent and summed in bfloat16 or wider, within the bound.
A program may use at most 128 MiB of HBM per device.

```python
import jax
import jax.numpy as jnp
from jax import lax

HEADS = 32
KV_HEADS = 8
HEAD_DIM = 128
PREFIX = 128
STEPS = 8
SEQ = 1024
TRAJ = 32


def draw_queries(key, part):
    key = jax.random.fold_in(key, 3)
    base = jnp.clip(jax.random.normal(key, (TRAJ, SEQ, HEADS * HEAD_DIM), jnp.float32), -4.0, 4.0)
    return base.astype(jnp.bfloat16)


def draw_keys(key, part):
    key = jax.random.fold_in(key, 4)
    base = jnp.clip(jax.random.normal(key, (TRAJ, SEQ, KV_HEADS * HEAD_DIM), jnp.float32), -4.0, 4.0)
    return base.astype(jnp.bfloat16)


def draw_boundaries(key, part):
    key = jax.random.fold_in(key, 6)
    widest = SEQ // (2 * STEPS)
    gaps = jax.random.randint(key, (TRAJ, STEPS - 1), 1, widest + 1)
    gaps = gaps.at[0].set(widest)
    starts = jnp.concatenate([jnp.zeros((TRAJ, 1), jnp.int32), jnp.cumsum(gaps, axis=1).astype(jnp.int32)], axis=1)
    return starts.astype(jnp.int32)


def draw_lengths(key, part):
    key = jax.random.fold_in(key, 7)
    drawn = jax.random.randint(key, (TRAJ,), SEQ // 2, SEQ + 1)
    return drawn.at[0].set(SEQ).astype(jnp.int32)


def shard_levels(own_key, shape, shards, least, high):
    loudness = 1.0
    for axis_at, shards_of in shards:
        heights = jax.random.uniform(jax.random.fold_in(jax.random.fold_in(own_key, 6), axis_at), (shards_of,), jnp.float32, least / len(shards), high / len(shards))
        loudness = loudness * jnp.repeat(jnp.exp(heights), shape[axis_at] // shards_of).reshape((-1,) + (1,) * (len(shape) - 1 - axis_at))
    return loudness


def noise(rng, shape, deviation, limit, shards=(), held_as=jnp.bfloat16):
    gain = shard_levels(rng, shape, shards, -0.22, 0.18) if shards else 1.0
    values = jax.random.normal(rng, shape, jnp.float32) * deviation * gain
    return jnp.minimum(jnp.maximum(values, -limit), limit).astype(held_as)


def setup_inputs(seed: int = 0) -> dict:
    streams_of = jax.random.split(jax.random.key(seed), 10)
    queries = draw_queries(jax.random.fold_in(streams_of[9], 71), 0)
    keys = draw_keys(jax.random.fold_in(streams_of[9], 71), 0)
    values = noise(streams_of[2], (TRAJ, SEQ, KV_HEADS * HEAD_DIM), 1.0, 6.0, ((0, 32), (1, 8)))
    prefix_keys = noise(streams_of[3], (PREFIX, KV_HEADS * HEAD_DIM), 1.0, 6.0)
    prefix_values = noise(streams_of[4], (PREFIX, KV_HEADS * HEAD_DIM), 1.0, 6.0)
    out_grad = noise(streams_of[5], (TRAJ, SEQ, HEADS * HEAD_DIM), 1.0, 6.0, ((0, 32), (1, 8)))
    boundaries = draw_boundaries(jax.random.fold_in(streams_of[9], 71), 0)
    lengths = draw_lengths(jax.random.fold_in(streams_of[9], 71), 0)
    advantages = noise(streams_of[8], (TRAJ, STEPS), 1.0, 4.0, ((0, 32),), jnp.float32)
    return dict(queries=queries, keys=keys, values=values, prefix_keys=prefix_keys, prefix_values=prefix_values, out_grad=out_grad, boundaries=boundaries, lengths=lengths, advantages=advantages)


NEG = -1e30


def masked_scores(query, key_rows, query_pos, key_pos, score_scale):
    scores = jnp.einsum('rgd,kd->grk', query.astype(jnp.float32), key_rows.astype(jnp.float32)) * score_scale
    seen = key_pos[None, :] <= query_pos[:, None]
    return jnp.where(seen[None], scores, NEG)


def block_grads(query, grad_out, key_rows, value_rows, query_pos, key_pos, score_scale):
    scores = masked_scores(query, key_rows, query_pos, key_pos, score_scale)
    peak = jnp.max(scores, axis=-1)
    raised = jnp.exp(scores - peak[..., None])
    total = jnp.sum(raised, axis=-1)
    attn_out = jnp.einsum('grk,kd->grd', raised.astype(jnp.bfloat16).astype(jnp.float32), value_rows.astype(jnp.float32)) / total[..., None]
    log_total = peak + jnp.log(total)
    delta = jnp.einsum('rgd,grd->gr', grad_out.astype(jnp.float32), attn_out)
    probs = jnp.exp(scores - log_total[..., None])
    probs_low = probs.astype(jnp.bfloat16).astype(jnp.float32)
    value_dot = jnp.einsum('rgd,kd->grk', grad_out.astype(jnp.float32), value_rows.astype(jnp.float32))
    score_grad = (probs * (value_dot - delta[..., None]) * score_scale).astype(jnp.bfloat16).astype(jnp.float32)
    query_grad = jnp.einsum('grk,kd->rgd', score_grad, key_rows.astype(jnp.float32))
    key_grad = jnp.einsum('grk,rgd->kd', score_grad, query.astype(jnp.float32))
    value_grad = jnp.einsum('grk,rgd->kd', probs_low, grad_out.astype(jnp.float32))
    return query_grad, key_grad, value_grad


def reference(queries, keys, values, prefix_keys, prefix_values, out_grad, boundaries, lengths, advantages):
    group = HEADS // KV_HEADS
    score_scale = HEAD_DIM ** -0.5
    position = jnp.arange(SEQ, dtype=jnp.int32)
    step_of = jnp.sum((boundaries[:, None, :] <= position[None, :, None]).astype(jnp.int32), axis=-1) - 1
    onehot = step_of[..., None] == jnp.arange(STEPS, dtype=jnp.int32)[None, None, :]
    token_weight = jnp.sum(jnp.where(onehot, advantages[:, None, :], 0.0), axis=-1)
    token_weight = jnp.where(position[None, :] < lengths[:, None], token_weight, 0.0)
    weighted_grad = (out_grad.astype(jnp.float32) * token_weight[..., None]).astype(jnp.bfloat16)
    prefix_k = prefix_keys.reshape(PREFIX, KV_HEADS, HEAD_DIM).transpose(1, 0, 2)
    prefix_v = prefix_values.reshape(PREFIX, KV_HEADS, HEAD_DIM).transpose(1, 0, 2)
    key_pos = jnp.concatenate([jnp.full((PREFIX,), -1, jnp.int32), position])
    block = SEQ // 8

    def one_traj(parts):
        query, grad_out, key_seq, value_seq = parts
        query_heads = query.reshape(SEQ, KV_HEADS, group, HEAD_DIM).transpose(1, 0, 2, 3)
        grad_heads = grad_out.reshape(SEQ, KV_HEADS, group, HEAD_DIM).transpose(1, 0, 2, 3)
        key_heads = jnp.concatenate([prefix_k, key_seq.reshape(SEQ, KV_HEADS, HEAD_DIM).transpose(1, 0, 2)], axis=1)
        value_heads = jnp.concatenate([prefix_v, value_seq.reshape(SEQ, KV_HEADS, HEAD_DIM).transpose(1, 0, 2)], axis=1)
        key_total = jnp.zeros((KV_HEADS, PREFIX + SEQ, HEAD_DIM), jnp.float32)
        value_total = jnp.zeros((KV_HEADS, PREFIX + SEQ, HEAD_DIM), jnp.float32)
        query_parts = []
        for index in range(8):
            lower = index * block
            upper = lower + block
            count = PREFIX + upper
            query_pos = position[lower:upper]

            def head_fn(qh, gh, kh, vh):
                return block_grads(qh, gh, kh, vh, query_pos, key_pos[:count], score_scale)

            query_part, key_part, value_part = jax.vmap(head_fn)(query_heads[:, lower:upper], grad_heads[:, lower:upper], key_heads[:, :count], value_heads[:, :count])
            query_parts.append(query_part)
            key_total = key_total.at[:, :count].add(key_part)
            value_total = value_total.at[:, :count].add(value_part)
        query_full = jnp.concatenate(query_parts, axis=1).transpose(1, 0, 2, 3).reshape(SEQ, HEADS * HEAD_DIM)
        key_flat = key_total.transpose(1, 0, 2).reshape(PREFIX + SEQ, KV_HEADS * HEAD_DIM)
        value_flat = value_total.transpose(1, 0, 2).reshape(PREFIX + SEQ, KV_HEADS * HEAD_DIM)
        return query_full.astype(jnp.bfloat16), key_flat, value_flat

    query_grad, key_flat, value_flat = lax.map(one_traj, (queries, weighted_grad, keys, values))
    key_grad = key_flat[:, PREFIX:].astype(jnp.bfloat16)
    value_grad = value_flat[:, PREFIX:].astype(jnp.bfloat16)
    prefix_key_grad = jnp.sum(key_flat[:, :PREFIX], axis=0)
    prefix_value_grad = jnp.sum(value_flat[:, :PREFIX], axis=0)
    return query_grad, key_grad, value_grad, prefix_key_grad, prefix_value_grad
```

```python
import functools

import jax
import jax.numpy as jnp
from jax import lax
from jax.experimental import pallas as pl
from jax.experimental.pallas import tpu as pltpu
from jax.sharding import PartitionSpec as P

HEADS = 32
KV_HEADS = 8
GROUP = HEADS // KV_HEADS
HEAD_DIM = 128
PREFIX = 128
ROWS = 128
STEPS = 8
SCALE = HEAD_DIM**-0.5
SCALE_LOG2 = SCALE * 1.4426950408889634
NEG = -1e30
MESH = pl.DeviceIdType.MESH
F32 = jnp.float32
BF16 = jnp.bfloat16
CONTRACT_LAST = (((1,), (1,)), ((), ()))
CONTRACT_FIRST = (((0,), (0,)), ((), ()))
CONTRACT_INNER = (((1,), (0,)), ((), ()))


def head_grads(h, ctx, keys_seen, unmasked, q_ref, og_ref, weight, kv, dkv, dq_ref, s_ref, d_ref):
    width = GROUP * HEAD_DIM
    cols = [pl.ds(pl.multiple_of(h * width + g * HEAD_DIM, HEAD_DIM), HEAD_DIM) for g in range(GROUP)]
    queries = jnp.concatenate([q_ref[:, c] for c in cols], axis=0)
    grads = jnp.concatenate(
        [(og_ref[:, c].astype(F32) * weight[...]).astype(BF16) for c in cols], axis=0
    )
    key_rows = kv[0, h, 0:keys_seen]
    value_rows = kv[1, h, 0:keys_seen]
    scores = lax.dot_general(key_rows, queries, CONTRACT_LAST, preferred_element_type=F32)
    query_pos = ctx * ROWS + lax.broadcasted_iota(jnp.int32, (1, ROWS), 1)
    query_pos = jnp.concatenate([query_pos] * GROUP, axis=1)
    key_pos = unmasked - PREFIX + lax.broadcasted_iota(jnp.int32, (keys_seen - unmasked, 1), 0)
    free, bound = scores[0:unmasked], scores[unmasked:]
    bound = jnp.where(key_pos <= query_pos, bound, NEG)
    s_ref[0:unmasked] = free
    s_ref[unmasked:keys_seen] = bound
    peak = jnp.maximum(
        jnp.max(free, axis=0, keepdims=True), jnp.max(bound, axis=0, keepdims=True)
    )
    d_ref[0:keys_seen] = lax.dot_general(value_rows, grads, CONTRACT_LAST, preferred_element_type=F32)
    raised = jnp.exp2((s_ref[0:keys_seen] - peak) * SCALE_LOG2)
    s_ref[0:keys_seen] = raised
    total = jnp.sum(raised, axis=0, keepdims=True)
    inverse = 1.0 / total
    delta = jnp.sum(raised * d_ref[0:keys_seen], axis=0, keepdims=True) * inverse
    probs = s_ref[0:keys_seen] * inverse
    score_grad = (probs * (d_ref[0:keys_seen] - delta)).astype(BF16)
    value_part = lax.dot_general(probs.astype(BF16), grads, CONTRACT_INNER, preferred_element_type=F32)
    dkv[1, h, 0:keys_seen] = value_part.astype(BF16)
    key_part = lax.dot_general(score_grad, queries, CONTRACT_INNER, preferred_element_type=F32)
    dkv[0, h, 0:keys_seen] = (key_part * SCALE).astype(BF16)
    query_part = lax.dot_general(key_rows, score_grad, CONTRACT_FIRST, preferred_element_type=F32)
    for g in range(GROUP):
        dq_ref[:, cols[g]] = (query_part[:, g * ROWS : (g + 1) * ROWS].T * SCALE).astype(BF16)


def kernel(
    q_ref, k_ref, v_ref, pk_ref, pv_ref, og_ref, bounds_ref, len_ref, adv_ref,
    dq_ref, dk_ref, dv_ref, dpk_ref, dpv_ref,
    kv, dkv, rb, zsum, s_ref, d_ref, weight,
    pbuf, acc, ybuf, part, zbuf, piece, part2, fin, pgb,
    kv_send, kv_recv, g_send, g_recv, p_send, p_recv,
    y_send, y_recv, z_send, z_recv, za_send, za_recv, ya_send, ya_recv, f_send, f_recv,
):
    dp = lax.axis_index("dp")
    ctx = lax.axis_index("ctx")
    y = ctx % 4
    hi = ctx // 4
    z = hi * 4 + dp // 8
    own = dp % 8
    base = dp - own

    def at_ctx(target):
        return (dp, target)

    def at_own(target):
        return (base + target, ctx)

    def at_z(target):
        return ((target % 4) * 8 + own, (target // 4) * 4 + y)

    barrier = pltpu.get_barrier_semaphore()
    for step in range(1, 8):
        pl.semaphore_signal(barrier, inc=1, device_id=at_ctx((ctx + step) % 8), device_id_type=MESH)
        pl.semaphore_signal(barrier, inc=1, device_id=at_own((own + step) % 8), device_id_type=MESH)
        if step != 4:
            pl.semaphore_signal(barrier, inc=1, device_id=at_z((z + step) % 8), device_id_type=MESH)

    def copy(src, dst, send, recv, target):
        return pltpu.make_async_remote_copy(
            src_ref=src, dst_ref=dst, send_sem=send, recv_sem=recv, device_id=target, device_id_type=MESH
        )

    def block(ref, h, j):
        return ref.at[:, h, pl.ds(pl.multiple_of((1 + j) * ROWS, ROWS), ROWS)]

    mine = pl.ds(pl.multiple_of((1 + ctx) * ROWS, ROWS), ROWS)
    for h in range(KV_HEADS):
        cols = slice(h * HEAD_DIM, (h + 1) * HEAD_DIM)
        kv[0, h, mine] = k_ref[:, cols]
        kv[1, h, mine] = v_ref[:, cols]
        kv[0, h, 0:PREFIX] = pk_ref[:, cols]
        kv[1, h, 0:PREFIX] = pv_ref[:, cols]
    for j in range(1, 8):

        @pl.when(jnp.logical_and(ctx < j, ctx // 4 == j // 4))
        def _(j=j):
            for h in range(KV_HEADS):
                kv[:, h, (1 + j) * ROWS : (2 + j) * ROWS] = jnp.zeros((2, ROWS, HEAD_DIM), BF16)

    pos = ctx * ROWS + lax.broadcasted_iota(jnp.int32, (ROWS, HEAD_DIM), 0)
    token = jnp.full((ROWS, HEAD_DIM), adv_ref[0, 0], F32)
    for s in range(1, STEPS):
        token = jnp.where(pos >= bounds_ref[0, s], adv_ref[0, s], token)
    weight[...] = jnp.where(pos < len_ref[0], token, 0.0)

    pl.semaphore_wait(barrier, 20)

    def own_copy(h, dy):
        target = hi * 4 + (y + dy) % 4
        return copy(
            block(kv, h, ctx), block(kv, h, ctx), kv_send.at[h, dy - 1], kv_recv.at[h, ctx], at_ctx(target)
        ), y + dy < 4

    def cross_copy(h):
        return copy(block(kv, h, ctx), block(kv, h, ctx), kv_send.at[h, 3], kv_recv.at[h, ctx], at_ctx(4 + y))

    def pass_copy(h, dy):
        return copy(
            block(kv, h, y), block(kv, h, y), kv_send.at[h, 2 + dy], kv_recv.at[h, y], at_ctx(4 + (y + dy) % 4)
        )

    def kv_arrived(h, j):
        copy(block(kv, h, j), block(kv, h, j), kv_send.at[h, 0], kv_recv.at[h, j], at_ctx(ctx)).wait_recv()

    def lo_term_copy(h, dy):
        target = (y + dy) % 4
        return copy(
            block(dkv, h, target), rb.at[3 - dy, :, h], g_send.at[h, dy - 1], g_recv.at[h, 3 - dy], at_ctx(4 + target)
        )

    def owner_term_copy(h, dy):
        target = (y + dy) % 4
        return copy(
            block(dkv, h, hi * 4 + target),
            rb.at[6 - dy, :, h],
            g_send.at[h, 2 + dy],
            g_recv.at[h, 6 - dy],
            at_ctx(hi * 4 + target),
        ), y + dy >= 4

    def back_copy(h):
        return copy(zsum.at[:, h], rb.at[0, :, h], g_send.at[h, 6], g_recv.at[h, 0], at_ctx(y))

    def term_arrived(h, slot):
        copy(zsum.at[:, h], rb.at[slot, :, h], g_send.at[h, 0], g_recv.at[h, slot], at_ctx(ctx)).wait_recv()

    def prefix_copy(h):
        slot = jnp.minimum((own - h + 7) % 8, 6)
        return copy(
            dkv.at[:, h, pl.ds(0, PREFIX)], pbuf.at[slot], p_send.at[h], p_recv.at[slot], at_own(h)
        ), own != h

    def when(pair, act):
        made, cond = pair
        pl.when(cond)(functools.partial(act, made))

    def start(made):
        made.start()

    def wait_send(made):
        made.wait_send()

    grads = functools.partial(
        head_grads, q_ref=q_ref, og_ref=og_ref, weight=weight, kv=kv, dkv=dkv, dq_ref=dq_ref, s_ref=s_ref, d_ref=d_ref
    )

    def send_terms(h):
        for dy in (1, 2, 3):
            when(owner_term_copy(h, dy), start)
        when(prefix_copy(h), start)

    @pl.when(hi == 0)
    def _():
        def send(h, c):
            cross_copy(h).start()
            for dy in (1, 2, 3):
                when(own_copy(h, dy), start)
            return c

        lax.fori_loop(0, KV_HEADS, send, 0)

        def step(h, c):
            for j in range(3):
                pl.when(j < ctx)(functools.partial(kv_arrived, h, j))
            grads(h, ctx, 5 * ROWS, PREFIX)
            send_terms(h)
            return c

        lax.fori_loop(0, KV_HEADS, step, 0)

    @pl.when(hi == 1)
    def _():
        def forward(h):
            for dy in (1, 2, 3):
                when(own_copy(h, dy), start)
            kv_arrived(h, y)
            for dy in (1, 2, 3):
                pass_copy(h, dy).start()

        def relay(h):
            for slot in range(3):
                term_arrived(h, slot)
            mine_too = dkv[:, h, pl.ds(pl.multiple_of((1 + y) * ROWS, ROWS), ROWS)].astype(F32)
            summed = mine_too + rb[0, :, h].astype(F32) + rb[1, :, h].astype(F32) + rb[2, :, h].astype(F32)
            zsum[:, h] = summed.astype(BF16)
            back_copy(h).start()

        forward(0)

        def step(h, c):
            pl.when(h + 1 < KV_HEADS)(lambda: forward(h + 1))
            for dy in (1, 2, 3):
                kv_arrived(h, (y + dy) % 4)
            for j in range(4, 7):
                pl.when(j < ctx)(functools.partial(kv_arrived, h, j))
            grads(h, ctx, 9 * ROWS, 5 * ROWS)
            for dy in (1, 2, 3):
                lo_term_copy(h, dy).start()
            send_terms(h)
            pl.when(h >= 1)(lambda: relay(h - 1))
            return c

        lax.fori_loop(0, KV_HEADS, step, 0)
        relay(KV_HEADS - 1)

    for slot in range(7):
        copy(pbuf.at[slot], pbuf.at[slot], p_send.at[0], p_recv.at[slot], at_own(own)).wait_recv()
    total = dkv[:, own, 0:PREFIX].astype(F32)
    for slot in range(7):
        total = total + pbuf[slot].astype(F32)
    acc[...] = total.reshape(2 * PREFIX, HEAD_DIM)

    def quarter(ref, i):
        return ref.at[pl.ds(pl.multiple_of(i * 64, 64), 64)]

    def eighth(ref, i):
        return ref.at[pl.ds(pl.multiple_of(i * 8, 8), 8)]

    ys = [
        copy(quarter(acc, (y + d) % 4), ybuf.at[3 - d], y_send.at[d - 1], y_recv.at[3 - d], at_ctx(hi * 4 + (y + d) % 4))
        for d in (1, 2, 3)
    ]
    for c in ys:
        c.start()
    for c in ys:
        c.wait_recv()
    part[...] = acc[pl.ds(pl.multiple_of(y * 64, 64), 64)] + ybuf[0] + ybuf[1] + ybuf[2]
    zs = [
        copy(eighth(part, (z + d) % 8), zbuf.at[7 - d], z_send.at[d - 1], z_recv.at[7 - d], at_z((z + d) % 8))
        for d in range(1, 8)
    ]
    for c in zs:
        c.start()
    for c in zs:
        c.wait_recv()
    total = part[pl.ds(pl.multiple_of(z * 8, 8), 8)]
    for slot in range(7):
        total = total + zbuf[slot]
    piece[...] = total
    part2[pl.ds(pl.multiple_of(z * 8, 8), 8)] = total
    zas = [
        copy(piece, eighth(part2, z), za_send.at[d - 1], za_recv.at[7 - d], at_z((z + d) % 8)) for d in range(1, 8)
    ]
    for c in zas:
        c.start()
    for d in range(1, 8):
        copy(piece, eighth(part2, (z + d) % 8), za_send.at[d - 1], za_recv.at[d - 1], at_z(z)).wait_recv()
    fin[pl.ds(pl.multiple_of(y * 64, 64), 64)] = part2[...]
    yas = [
        copy(part2, quarter(fin, y), ya_send.at[d - 1], ya_recv.at[3 - d], at_ctx(hi * 4 + (y + d) % 4))
        for d in (1, 2, 3)
    ]
    for c in yas:
        c.start()
    for d in (1, 2, 3):
        copy(part2, quarter(fin, (y + d) % 4), ya_send.at[d - 1], ya_recv.at[d - 1], at_ctx(ctx)).wait_recv()
    pgb[own] = fin[...].astype(BF16)
    fs = [
        copy(pgb.at[own], pgb.at[own], f_send.at[d - 1], f_recv.at[7 - d], at_own((own + d) % 8)) for d in range(1, 8)
    ]
    for c in fs:
        c.start()

    @pl.when(hi == 0)
    def _():
        def finish(h, c):
            term_arrived(h, 0)
            return c

        lax.fori_loop(0, KV_HEADS, finish, 0)

    @pl.when(hi == 1)
    def _():
        rb[0] = jnp.zeros(rb.shape[1:], BF16)

    for dy in (1, 2, 3):

        @pl.when(y + dy < 4)
        def _(dy=dy):
            def finish(h, c):
                term_arrived(h, 2 + dy)
                return c

            lax.fori_loop(0, KV_HEADS, finish, 0)

        @pl.when(y + dy >= 4)
        def _(dy=dy):
            rb[2 + dy] = jnp.zeros(rb.shape[1:], BF16)

    for h in range(KV_HEADS):
        total = dkv[:, h, mine].astype(F32)
        for slot in (0, 3, 4, 5):
            total = total + rb[slot, :, h].astype(F32)
        cols = slice(h * HEAD_DIM, (h + 1) * HEAD_DIM)
        dk_ref[:, cols] = total[0].astype(BF16)
        dv_ref[:, cols] = total[1].astype(BF16)

    for d in range(1, 8):
        there = (own + d) % 8
        copy(pgb.at[there], pgb.at[there], f_send.at[0], f_recv.at[d - 1], at_own(own)).wait_recv()
    for h in range(KV_HEADS):
        cols = slice(h * HEAD_DIM, (h + 1) * HEAD_DIM)
        dpk_ref[:, cols] = pgb[h, 0:PREFIX].astype(F32)
        dpv_ref[:, cols] = pgb[h, PREFIX:].astype(F32)

    for c in ys + zs + zas + yas + fs:
        c.wait_send()

    def drain(h, c):
        for dy in (1, 2, 3):
            when(own_copy(h, dy), wait_send)
            when(owner_term_copy(h, dy), wait_send)
        when(prefix_copy(h), wait_send)

        @pl.when(hi == 0)
        def _():
            cross_copy(h).wait_send()

        @pl.when(hi == 1)
        def _():
            for dy in (1, 2, 3):
                pass_copy(h, dy).wait_send()
                lo_term_copy(h, dy).wait_send()
            back_copy(h).wait_send()

        return c

    lax.fori_loop(0, KV_HEADS, drain, 0)


def body(queries, keys, values, prefix_keys, prefix_values, out_grad, boundaries, lengths, advantages):
    width, kv_width = queries.shape[2], keys.shape[2]
    vmem = pl.BlockSpec(memory_space=pltpu.VMEM)
    smem = pl.BlockSpec(memory_space=pltpu.SMEM)
    dma = pltpu.SemaphoreType.DMA
    key_rows = PREFIX + 8 * ROWS
    outs = pl.pallas_call(
        kernel,
        out_shape=[
            jax.ShapeDtypeStruct((ROWS, width), BF16),
            jax.ShapeDtypeStruct((ROWS, kv_width), BF16),
            jax.ShapeDtypeStruct((ROWS, kv_width), BF16),
            jax.ShapeDtypeStruct((PREFIX, kv_width), F32),
            jax.ShapeDtypeStruct((PREFIX, kv_width), F32),
        ],
        in_specs=[vmem] * 6 + [smem] * 3,
        out_specs=[vmem] * 5,
        scratch_shapes=[
            pltpu.VMEM((2, KV_HEADS, key_rows, HEAD_DIM), BF16),
            pltpu.VMEM((2, KV_HEADS, key_rows, HEAD_DIM), BF16),
            pltpu.VMEM((6, 2, KV_HEADS, ROWS, HEAD_DIM), BF16),
            pltpu.VMEM((2, KV_HEADS, ROWS, HEAD_DIM), BF16),
            pltpu.VMEM((key_rows, GROUP * ROWS), F32),
            pltpu.VMEM((key_rows, GROUP * ROWS), F32),
            pltpu.VMEM((ROWS, HEAD_DIM), F32),
            pltpu.VMEM((7, 2, PREFIX, HEAD_DIM), BF16),
            pltpu.VMEM((2 * PREFIX, HEAD_DIM), F32),
            pltpu.VMEM((3, 64, HEAD_DIM), F32),
            pltpu.VMEM((64, HEAD_DIM), F32),
            pltpu.VMEM((7, 8, HEAD_DIM), F32),
            pltpu.VMEM((8, HEAD_DIM), F32),
            pltpu.VMEM((64, HEAD_DIM), F32),
            pltpu.VMEM((2 * PREFIX, HEAD_DIM), F32),
            pltpu.VMEM((KV_HEADS, 2 * PREFIX, HEAD_DIM), BF16),
            dma((KV_HEADS, 6)),
            dma((KV_HEADS, 8)),
            dma((KV_HEADS, 7)),
            dma((KV_HEADS, 6)),
            dma((KV_HEADS,)),
            dma((7,)),
            dma((3,)),
            dma((3,)),
            dma((7,)),
            dma((7,)),
            dma((7,)),
            dma((7,)),
            dma((3,)),
            dma((3,)),
            dma((7,)),
            dma((7,)),
        ],
        compiler_params=pltpu.CompilerParams(
            collective_id=0, has_side_effects=True, vmem_limit_bytes=56 * 2**20
        ),
        cost_estimate=pl.CostEstimate(flops=6 * 10**9, bytes_accessed=6 * 10**6, transcendentals=5 * 10**6),
        name="grads",
    )(
        queries[0], keys[0], values[0], prefix_keys, prefix_values, out_grad[0], boundaries, lengths, advantages
    )
    return outs[0][None], outs[1][None], outs[2][None], outs[3], outs[4]


def solution(mesh):
    in_specs = (
        P("dp", "ctx", None),
        P("dp", "ctx", None),
        P("dp", "ctx", None),
        P(),
        P(),
        P("dp", "ctx", None),
        P("dp", None),
        P("dp"),
        P("dp", None),
    )
    out_specs = (P("dp", "ctx", None), P("dp", "ctx", None), P("dp", "ctx", None), P(), P())
    return jax.shard_map(body, mesh=mesh, in_specs=in_specs, out_specs=out_specs, check_vma=False)
```

```python
import functools

import jax
import jax.numpy as jnp
from jax import lax
from jax.experimental import pallas as pl
from jax.experimental.pallas import tpu as pltpu
from jax.sharding import PartitionSpec as P

HEADS = 32
KV_HEADS = 8
GROUP = HEADS // KV_HEADS
HEAD_DIM = 128
PREFIX = 128
ROWS = 128
STEPS = 8
SCALE = HEAD_DIM**-0.5
SCALE_LOG2 = SCALE * 1.4426950408889634
NEG = -1e30
MESH = pl.DeviceIdType.MESH
F32 = jnp.float32
BF16 = jnp.bfloat16
AHEAD = 3
SECOND = 1
BACK = 2
LAG = 4
OVER = (1, 3, 5, 7)
WINDOW = 3
EARLY = 4
TAIL = 7
CONTRACT_LAST = (((1,), (1,)), ((), ()))
CONTRACT_FIRST = (((0,), (0,)), ((), ()))
CONTRACT_INNER = (((1,), (0,)), ((), ()))


def head_grads(h, ctx, keys_seen, unmasked, q_ref, og_ref, weight, kv, dkv, dq_ref, s_ref, d_ref):
    width = GROUP * HEAD_DIM
    cols = [pl.ds(pl.multiple_of(h * width + g * HEAD_DIM, HEAD_DIM), HEAD_DIM) for g in range(GROUP)]
    queries = jnp.concatenate([q_ref[:, c] for c in cols], axis=0)
    grads = jnp.concatenate(
        [(og_ref[:, c].astype(F32) * weight[...]).astype(BF16) for c in cols], axis=0
    )
    key_rows = kv[0, h, 0:keys_seen]
    value_rows = kv[1, h, 0:keys_seen]
    scores = lax.dot_general(key_rows, queries, CONTRACT_LAST, preferred_element_type=F32)
    query_pos = ctx * ROWS + lax.broadcasted_iota(jnp.int32, (1, ROWS), 1)
    query_pos = jnp.concatenate([query_pos] * GROUP, axis=1)
    key_pos = unmasked - PREFIX + lax.broadcasted_iota(jnp.int32, (keys_seen - unmasked, 1), 0)
    free, bound = scores[0:unmasked], scores[unmasked:]
    bound = jnp.where(key_pos <= query_pos, bound, NEG)
    s_ref[0:unmasked] = free
    s_ref[unmasked:keys_seen] = bound
    peak = jnp.maximum(
        jnp.max(free, axis=0, keepdims=True), jnp.max(bound, axis=0, keepdims=True)
    )
    d_ref[0:keys_seen] = lax.dot_general(value_rows, grads, CONTRACT_LAST, preferred_element_type=F32)
    raised = jnp.exp2((s_ref[0:keys_seen] - peak) * SCALE_LOG2)
    s_ref[0:keys_seen] = raised
    total = jnp.sum(raised, axis=0, keepdims=True)
    inverse = 1.0 / total
    delta = jnp.sum(raised * d_ref[0:keys_seen], axis=0, keepdims=True) * inverse
    probs = s_ref[0:keys_seen] * inverse
    score_grad = (probs * (d_ref[0:keys_seen] - delta)).astype(BF16)
    value_part = lax.dot_general(probs.astype(BF16), grads, CONTRACT_INNER, preferred_element_type=F32)
    dkv[1, h, 0:keys_seen] = value_part.astype(BF16)
    key_part = lax.dot_general(score_grad, queries, CONTRACT_INNER, preferred_element_type=F32)
    dkv[0, h, 0:keys_seen] = (key_part * SCALE).astype(BF16)
    query_part = lax.dot_general(key_rows, score_grad, CONTRACT_FIRST, preferred_element_type=F32)
    for g in range(GROUP):
        dq_ref[:, cols[g]] = (query_part[:, g * ROWS : (g + 1) * ROWS].T * SCALE).astype(BF16)


def kernel(
    q_hbm, k_hbm, v_hbm, pk_hbm, pv_hbm, og_hbm, bounds_ref, len_ref, adv_ref,
    dq_hbm, dk_hbm, dv_hbm, pg_hbm,
    q_ref, og_ref, dq_ref, dk_ref, dv_ref,
    kv, dkv, rb, s_ref, d_ref, weight,
    pbuf, acc, zbuf, ybuf, piece, fin, pgb,
    in_sem, kv_in_sem, out_sem, dq_sem, dkv_sem,
    kv_send, kv_recv, kv_recv_v, g_send, g_recv, p_send, p_recv,
    z_send, z_recv, y_send, y_recv, za_send, za_recv, f_send, f_recv,
):
    dp = lax.axis_index("dp")
    ctx = lax.axis_index("ctx")
    y = ctx % 4
    hi = ctx // 4
    z = hi * 4 + dp // 8
    own = dp % 8
    base = dp - own
    up = (y + 1) % 4
    down = (y + 3) % 4
    far = (y + 2) % 4

    def at_ctx(target):
        return (dp, target)

    def at_hi(target):
        return (dp, 4 + target)

    def at_own(target):
        return (base + target, ctx)

    def at_z(target):
        return ((target % 4) * 8 + own, (target // 4) * 4 + y)

    barrier = pltpu.get_barrier_semaphore()
    for step in range(1, 8):
        pl.semaphore_signal(barrier, inc=1, device_id=at_ctx((ctx + step) % 8), device_id_type=MESH)
        pl.semaphore_signal(barrier, inc=1, device_id=at_own((own + step) % 8), device_id_type=MESH)
        if step != 4:
            pl.semaphore_signal(barrier, inc=1, device_id=at_z((z + step) % 8), device_id_type=MESH)

    mine = pl.ds(pl.multiple_of((1 + ctx) * ROWS, ROWS), ROWS)
    kv_in = []
    for h in range(KV_HEADS):
        cols = pl.ds(h * HEAD_DIM, HEAD_DIM)
        pairs = (
            (k_hbm.at[:, cols], kv.at[0, h, mine]),
            (v_hbm.at[:, cols], kv.at[1, h, mine]),
            (pk_hbm.at[:, cols], kv.at[0, h, pl.ds(0, PREFIX)]),
            (pv_hbm.at[:, cols], kv.at[1, h, pl.ds(0, PREFIX)]),
        )
        for i, (s, d) in enumerate(pairs):
            kv_in.append(pltpu.make_async_copy(s, d, kv_in_sem.at[h, i]))
    for c in kv_in:
        c.start()
    big_in = [
        pltpu.make_async_copy(q_hbm, q_ref, in_sem.at[0]),
        pltpu.make_async_copy(og_hbm, og_ref, in_sem.at[1]),
    ]
    for c in big_in:
        c.start()

    def copy(src, dst, send, recv, target):
        return pltpu.make_async_remote_copy(
            src_ref=src, dst_ref=dst, send_sem=send, recv_sem=recv, device_id=target, device_id_type=MESH
        )

    def rows_of(j):
        return pl.ds(pl.multiple_of((1 + j) * ROWS, ROWS), ROWS)

    def block(ref, h, j):
        return ref.at[:, h, rows_of(j)]

    def half(ref, side, h, j):
        return ref.at[side, h, rows_of(j)]

    for j in range(1, 8):

        @pl.when(jnp.logical_and(ctx < j, hi == j // 4))
        def _(j=j):
            for h in range(KV_HEADS):
                kv[:, h, (1 + j) * ROWS : (2 + j) * ROWS] = jnp.zeros((2, ROWS, HEAD_DIM), BF16)

    pos = ctx * ROWS + lax.broadcasted_iota(jnp.int32, (ROWS, HEAD_DIM), 0)
    token = jnp.full((ROWS, HEAD_DIM), adv_ref[0, 0], F32)
    for s in range(1, STEPS):
        token = jnp.where(pos >= bounds_ref[0, s], adv_ref[0, s], token)
    weight[...] = jnp.where(pos < len_ref[0], token, 0.0)
    for c in kv_in:
        c.wait()
    for c in big_in:
        c.wait()

    pl.semaphore_wait(barrier, 20)

    def full_kv(kind, j, target):
        return lambda h: copy(block(kv, h, j), block(kv, h, j), kv_send.at[h, kind], kv_recv.at[h, j], target)

    def key_half(kind, j, target):
        return lambda h: copy(half(kv, 0, h, j), half(kv, 0, h, j), kv_send.at[h, kind], kv_recv.at[h, j], target)

    def value_half(kind, j, target):
        return lambda h: copy(half(kv, 1, h, j), half(kv, 1, h, j), kv_send.at[h, kind], kv_recv_v.at[h, j], target)

    lo_own = [(y + d < 4, full_kv(d - 1, ctx, at_ctx((y + d) % 4))) for d in (1, 2, 3)]
    lo_cross = [(None, full_kv(3, ctx, at_hi(y)))]
    hi_own = [
        (y < 3, full_kv(0, ctx, at_hi(up))),
        (y == 0, full_kv(1, ctx, at_hi(3))),
    ]
    hi_near = [(None, full_kv(2, y, at_hi(up))), (None, full_kv(3, y, at_hi(down)))]
    hi_pass_down = [
        (jnp.logical_or(y == 0, y == 1), full_kv(4, down, at_hi(up))),
        (y == 3, key_half(4, down, at_hi(up))),
    ]
    hi_pass_up = [
        (y == 0, full_kv(5, up, at_hi(down))),
        (y == 1, value_half(5, up, at_hi(down))),
    ]
    hi_pass_own = [
        (y == 1, key_half(6, 4 + down, at_hi(up))),
        (y == 2, full_kv(6, 4 + down, at_hi(up))),
        (y == 3, value_half(7, 4 + up, at_hi(down))),
    ]
    hi_pass = hi_pass_down + hi_pass_up + hi_pass_own

    def full_term(kind, j, slot, sem, target):
        return lambda h: copy(block(dkv, h, j), rb.at[slot, :, h], g_send.at[h, kind], g_recv.at[h, sem], target)

    def half_term(kind, side, j, slot, sem, target):
        return lambda h: copy(
            half(dkv, side, h, j), rb.at[slot, side, h], g_send.at[h, kind], g_recv.at[h, sem], target
        )

    lo_terms = [
        (y + d >= 4, full_term(d - 1, (y + d) % 4, 4 - d, 4 - d, at_ctx((y + d) % 4))) for d in (1, 2, 3)
    ]
    hi_first = [
        (y == 0, half_term(0, 0, far, 4, 4, at_hi(up))),
        (y == 0, half_term(1, 1, far, 4, 5, at_hi(down))),
        (y == 1, full_term(0, far, 4, 4, at_hi(down))),
        (y == 2, full_term(0, far, 6, 8, at_hi(down))),
        (y == 3, full_term(0, far, 5, 6, at_hi(up))),
        (y == 2, half_term(2, 0, 4 + far, 5, 6, at_hi(up))),
        (y == 2, half_term(3, 1, 4 + far, 5, 7, at_hi(down))),
        (y == 3, full_term(2, 4 + far, 4, 4, at_hi(down))),
        (y == 3, full_term(5, 4 + down, 2, 2, at_hi(down))),
    ]
    to_up = [(None, full_term(6, up, 0, 0, at_hi(up)))]
    to_down = [(None, full_term(7, down, 1, 1, at_hi(down)))]
    own_up = [(y == 3, full_term(8, 4 + up, 3, 3, at_hi(up)))]
    own_down = [(jnp.logical_or(y == 1, y == 2), full_term(5, 4 + down, 2, 2, at_hi(down)))]
    hi_second = to_up + to_down + own_up + own_down
    hi_back = [(None, full_term(9, y, 0, 0, at_ctx(y)))]

    def prefix_made(h):
        slot = jnp.minimum((own - h + 7) % 8, 6)
        return copy(dkv.at[:, h, pl.ds(0, PREFIX)], pbuf.at[slot], p_send.at[h], p_recv.at[slot], at_own(h))

    def start(entries, h):
        for cond, make in entries:
            if cond is None:
                make(h).start()
            else:
                pl.when(cond)(lambda make=make: make(h).start())

    def wait_send(entries, h):
        for cond, make in entries:
            if cond is None:
                make(h).wait_send()
            else:
                pl.when(cond)(lambda make=make: make(h).wait_send())

    def kv_arrived(h, j):
        copy(block(kv, h, j), block(kv, h, j), kv_send.at[h, 0], kv_recv.at[h, j], at_ctx(ctx)).wait_recv()

    def halves_arrived(h, j):
        copy(half(kv, 0, h, j), half(kv, 0, h, j), kv_send.at[h, 0], kv_recv.at[h, j], at_ctx(ctx)).wait_recv()
        copy(half(kv, 1, h, j), half(kv, 1, h, j), kv_send.at[h, 0], kv_recv_v.at[h, j], at_ctx(ctx)).wait_recv()

    def term_arrived(h, slot, sem=None):
        sem = slot if sem is None else sem
        copy(rb.at[slot, :, h], rb.at[slot, :, h], g_send.at[h, 0], g_recv.at[h, sem], at_ctx(ctx)).wait_recv()

    def half_term_arrived(h, slot, side, sem):
        copy(
            rb.at[slot, side, h], rb.at[slot, side, h], g_send.at[h, 0], g_recv.at[h, sem], at_ctx(ctx)
        ).wait_recv()

    grads = functools.partial(
        head_grads, q_ref=q_ref, og_ref=og_ref, weight=weight, kv=kv, dkv=dkv, dq_ref=dq_ref, s_ref=s_ref, d_ref=d_ref
    )

    def dq_copy(h):
        cols = pl.ds(pl.multiple_of(h * GROUP * HEAD_DIM, HEAD_DIM), GROUP * HEAD_DIM)
        return pltpu.make_async_copy(dq_ref.at[:, cols], dq_hbm.at[:, cols], dq_sem.at[h])

    def dkv_copies(h):
        cols = pl.ds(pl.multiple_of(h * HEAD_DIM, HEAD_DIM), HEAD_DIM)
        return (
            pltpu.make_async_copy(dk_ref.at[:, cols], dk_hbm.at[:, cols], dkv_sem.at[h, 0]),
            pltpu.make_async_copy(dv_ref.at[:, cols], dv_hbm.at[:, cols], dkv_sem.at[h, 1]),
        )

    def after_grads(h):
        pl.when(own != h)(lambda: prefix_made(h).start())
        dq_copy(h).start()

    def finish(h):
        def store(total):
            cols = pl.ds(pl.multiple_of(h * HEAD_DIM, HEAD_DIM), HEAD_DIM)
            dk_ref[:, cols] = total[0].astype(BF16)
            dv_ref[:, cols] = total[1].astype(BF16)
            for c in dkv_copies(h):
                c.start()

        @pl.when(hi == 0)
        def _():
            term_arrived(h, 0)
            for d in (1, 2, 3):

                @pl.when(y + d < 4)
                def _(d=d):
                    term_arrived(h, d)

                @pl.when(y + d >= 4)
                def _(d=d):
                    rb[d, :, h] = jnp.zeros((2, ROWS, HEAD_DIM), BF16)

            total = dkv[:, h, mine].astype(F32)
            for slot in range(4):
                total = total + rb[slot, :, h].astype(F32)
            store(total)

        @pl.when(hi == 1)
        def _():
            @pl.when(y < 3)
            def _():
                term_arrived(h, 2)

            @pl.when(y == 3)
            def _():
                rb[2, :, h] = jnp.zeros((2, ROWS, HEAD_DIM), BF16)

            @pl.when(y == 0)
            def _():
                term_arrived(h, 3)

            @pl.when(y > 0)
            def _():
                rb[3, :, h] = jnp.zeros((2, ROWS, HEAD_DIM), BF16)

            store(dkv[:, h, mine].astype(F32) + rb[2, :, h].astype(F32) + rb[3, :, h].astype(F32))

    def eighth(ref, i):
        return ref.at[pl.ds(pl.multiple_of(i * 32, 32), 32)]

    z_out = [
        lambda d=d: copy(eighth(acc, (z + d) % 8), zbuf.at[7 - d], z_send.at[d - 1], z_recv.at[7 - d], at_z((z + d) % 8))
        for d in range(1, 8)
    ]
    y_out = [
        lambda d=d: copy(ybuf.at[y], ybuf.at[y], y_send.at[d - 1], y_recv.at[3 - d], at_ctx(hi * 4 + (y + d) % 4))
        for d in range(1, 4)
    ]
    za_out = [
        lambda d=d: copy(piece, eighth(fin, z), za_send.at[d - 1], za_recv.at[7 - d], at_z((z + d) % 8))
        for d in range(1, 8)
    ]
    f_out = [
        lambda d=d: copy(pgb.at[own], pgb.at[own], f_send.at[d - 1], f_recv.at[7 - d], at_own((own + d) % 8))
        for d in range(1, 8)
    ]

    def prefix_steps(t):
        @pl.when(t - own == OVER[0])
        def _():
            for slot in range(7):
                copy(pbuf.at[slot], pbuf.at[slot], p_send.at[0], p_recv.at[slot], at_own(own)).wait_recv()
            total = dkv[:, own, 0:PREFIX].astype(F32)
            for slot in range(7):
                total = total + pbuf[slot].astype(F32)
            acc[...] = total.reshape(2 * PREFIX, HEAD_DIM)
            for c in z_out:
                c().start()

        @pl.when(t - own == OVER[1])
        def _():
            for slot in range(7):
                copy(zbuf.at[slot], zbuf.at[slot], z_send.at[0], z_recv.at[slot], at_z(z)).wait_recv()
            total = acc[pl.ds(pl.multiple_of(z * 32, 32), 32)]
            for slot in range(7):
                total = total + zbuf[slot]
            ybuf[y] = total
            for c in y_out:
                c().start()

        @pl.when(t - own == OVER[2])
        def _():
            for d in (1, 2, 3):
                there = (y + d) % 4
                copy(ybuf.at[there], ybuf.at[there], y_send.at[0], y_recv.at[d - 1], at_ctx(ctx)).wait_recv()
            total = ((ybuf[0] + ybuf[1]) + ybuf[2]) + ybuf[3]
            piece[...] = total
            fin[pl.ds(pl.multiple_of(z * 32, 32), 32)] = total
            for c in za_out:
                c().start()

        @pl.when(t - own == OVER[3])
        def _():
            for d in range(1, 8):
                copy(piece, eighth(fin, (z + d) % 8), za_send.at[0], za_recv.at[d - 1], at_z(z)).wait_recv()
            pgb[own] = fin[...].astype(BF16)
            for c in f_out:
                c().start()

    def near(h):
        if EARLY == 0:
            start(hi_own, h)
        else:
            pl.when(h >= EARLY)(lambda: start(hi_own, h))
        kv_arrived(h, y)
        start(hi_near, h)

    def pass_on(h):
        kv_arrived(h, down)
        start(hi_pass_down, h)
        kv_arrived(h, up)
        start(hi_pass_up, h)
        pl.when(jnp.logical_or(y == 1, y == 2))(lambda: kv_arrived(h, 4 + down))
        pl.when(y == 3)(lambda: kv_arrived(h, 4))
        start(hi_pass_own, h)

    def all_here(h):
        pl.when(y == 0)(lambda: halves_arrived(h, far))
        pl.when(y > 0)(lambda: kv_arrived(h, far))
        pl.when(y == 2)(lambda: halves_arrived(h, 4))
        pl.when(y == 3)(lambda: kv_arrived(h, 5))
        pl.when(y == 3)(lambda: kv_arrived(h, 6))

    def add_half(side, h, j, slot, sem):
        half_term_arrived(h, slot, side, sem)
        rows = rows_of(j)
        dkv[side, h, rows] = (dkv[side, h, rows].astype(F32) + rb[slot, side, h].astype(F32)).astype(BF16)

    def add_full(h, j, slot, sem):
        term_arrived(h, slot, sem)
        rows = rows_of(j)
        dkv[:, h, rows] = (dkv[:, h, rows].astype(F32) + rb[slot, :, h].astype(F32)).astype(BF16)

    def first(h):
        start(hi_first, h)
        pl.when(y >= 2)(lambda: start(to_up, h))
        pl.when(y == 2)(lambda: start(to_down, h))

    def second(h):
        @pl.when(y == 0)
        def _():
            add_full(h, down, 4, 4)
            start(to_down, h)
            add_full(h, up, 5, 6)
            start(to_up, h)

        @pl.when(y == 1)
        def _():
            add_full(h, down, 6, 8)
            start(to_down, h)
            add_half(0, h, up, 4, 4)
            start(to_up, h)
            add_half(1, h, 4 + down, 5, 7)
            start(own_down, h)

        @pl.when(y == 2)
        def _():
            add_full(h, 4 + down, 4, 4)
            start(own_down, h)

        @pl.when(y == 3)
        def _():
            add_half(1, h, down, 4, 5)
            start(to_down, h)
            add_half(0, h, 4 + up, 5, 6)
            start(own_up, h)

    def back(h):
        term_arrived(h, 0)
        term_arrived(h, 1)
        rows = rows_of(y)
        total = dkv[:, h, rows].astype(F32) + rb[0, :, h].astype(F32) + rb[1, :, h].astype(F32)
        dkv[:, h, rows] = total.astype(BF16)
        start(hi_back, h)

    @pl.when(hi == 0)
    def _():
        for h in range(WINDOW):
            start(lo_cross, h)
        for h in range(KV_HEADS):
            start(lo_own, h)
        for h in range(WINDOW, KV_HEADS):
            wait_send(lo_cross, h - WINDOW)
            start(lo_cross, h)

    @pl.when(hi == 1)
    def _():
        for h in range(EARLY):
            start(hi_own, h)
        for h in range(AHEAD):
            near(h)
        for h in range(AHEAD - 1):
            pass_on(h)

    def step(t, c):
        @pl.when(jnp.logical_and(hi == 0, t < KV_HEADS))
        def _():
            for j in range(3):
                pl.when(j < ctx)(lambda j=j: kv_arrived(t, j))
            grads(t, ctx, 5 * ROWS, PREFIX)
            start(lo_terms, t)
            after_grads(t)

        @pl.when(hi == 1)
        def _():
            pl.when(t + AHEAD < KV_HEADS)(lambda: near(t + AHEAD))
            pl.when(t + AHEAD - 1 < KV_HEADS)(lambda: pass_on(t + AHEAD - 1))

            @pl.when(t < KV_HEADS)
            def _():
                all_here(t)
                grads(t, ctx, 9 * ROWS, 5 * ROWS)
                first(t)
                after_grads(t)

            pl.when(jnp.logical_and(t >= SECOND, t - SECOND < KV_HEADS))(lambda: second(t - SECOND))
            pl.when(jnp.logical_and(t >= BACK, t - BACK < KV_HEADS))(lambda: back(t - BACK))

        prefix_steps(t)
        pl.when(jnp.logical_and(t >= LAG, t - LAG < KV_HEADS))(lambda: finish(t - LAG))
        return c

    lax.fori_loop(0, KV_HEADS + TAIL, step, 0)

    for d in range(1, 8):
        there = (own + d) % 8
        copy(pgb.at[there], pgb.at[there], f_send.at[0], f_recv.at[d - 1], at_own(own)).wait_recv()
    out = pltpu.make_async_copy(pgb, pg_hbm, out_sem.at[0])
    out.start()

    for c in z_out + y_out + za_out + f_out:
        c().wait_send()

    def drain(h, c):
        pl.when(own != h)(lambda: prefix_made(h).wait_send())

        @pl.when(hi == 0)
        def _():
            wait_send(lo_own + lo_terms, h)
            pl.when(h >= KV_HEADS - WINDOW)(lambda: wait_send(lo_cross, h))

        @pl.when(hi == 1)
        def _():
            wait_send(hi_own + hi_near + hi_pass + hi_first + hi_second + hi_back, h)

        dq_copy(h).wait()
        for made in dkv_copies(h):
            made.wait()
        return c

    lax.fori_loop(0, KV_HEADS, drain, 0)
    out.wait()


def place_kernel(dq_in, dk_in, dv_in, pg_ref, dq_out, dk_out, dv_out, dpk_ref, dpv_ref, big, small, in_sem, out_sem):
    parts = []
    for i in range(4):
        rows = pl.ds(i * 32, 32)
        parts.append((dq_in.at[rows], big.at[rows], dq_out.at[rows]))
    parts.append((dk_in, small.at[0], dk_out))
    parts.append((dv_in, small.at[1], dv_out))
    loads = [pltpu.make_async_copy(s, m, in_sem.at[i]) for i, (s, m, d) in enumerate(parts)]
    stores = [pltpu.make_async_copy(m, d, out_sem.at[i]) for i, (s, m, d) in enumerate(parts)]
    for c in loads:
        c.start()
    for h in range(KV_HEADS):
        cols = slice(h * HEAD_DIM, (h + 1) * HEAD_DIM)
        dpk_ref[:, cols] = pg_ref[h, 0:PREFIX].astype(F32)
        dpv_ref[:, cols] = pg_ref[h, PREFIX:].astype(F32)
    for load, store in zip(loads, stores):
        load.wait()
        store.start()
    for c in stores:
        c.wait()


def body(queries, keys, values, prefix_keys, prefix_values, out_grad, boundaries, lengths, advantages):
    width, kv_width = queries.shape[2], keys.shape[2]
    vmem = pl.BlockSpec(memory_space=pltpu.VMEM)
    smem = pl.BlockSpec(memory_space=pltpu.SMEM)
    any_ = pl.BlockSpec(memory_space=pl.ANY)
    dma = pltpu.SemaphoreType.DMA
    key_rows = PREFIX + 8 * ROWS
    pair = (2, KV_HEADS, key_rows, HEAD_DIM)
    shapes = [
        jax.ShapeDtypeStruct((ROWS, width), BF16),
        jax.ShapeDtypeStruct((ROWS, kv_width), BF16),
        jax.ShapeDtypeStruct((ROWS, kv_width), BF16),
    ]
    prefix_shape = jax.ShapeDtypeStruct((PREFIX, kv_width), F32)
    outs = pl.pallas_call(
        kernel,
        out_shape=shapes + [jax.ShapeDtypeStruct((KV_HEADS, 2 * PREFIX, HEAD_DIM), BF16)],
        in_specs=[any_] * 6 + [smem] * 3,
        out_specs=[any_] * 4,
        scratch_shapes=[
            pltpu.VMEM((ROWS, width), BF16),
            pltpu.VMEM((ROWS, width), BF16),
            pltpu.VMEM((ROWS, width), BF16),
            pltpu.VMEM((ROWS, kv_width), BF16),
            pltpu.VMEM((ROWS, kv_width), BF16),
            pltpu.VMEM(pair, BF16),
            pltpu.VMEM(pair, BF16),
            pltpu.VMEM((7, 2, KV_HEADS, ROWS, HEAD_DIM), BF16),
            pltpu.VMEM((key_rows, GROUP * ROWS), F32),
            pltpu.VMEM((key_rows, GROUP * ROWS), F32),
            pltpu.VMEM((ROWS, HEAD_DIM), F32),
            pltpu.VMEM((7, 2, PREFIX, HEAD_DIM), BF16),
            pltpu.VMEM((2 * PREFIX, HEAD_DIM), F32),
            pltpu.VMEM((7, 32, HEAD_DIM), F32),
            pltpu.VMEM((4, 32, HEAD_DIM), F32),
            pltpu.VMEM((32, HEAD_DIM), F32),
            pltpu.VMEM((2 * PREFIX, HEAD_DIM), F32),
            pltpu.VMEM((KV_HEADS, 2 * PREFIX, HEAD_DIM), BF16),
            dma((2,)),
            dma((KV_HEADS, 4)),
            dma((1,)),
            dma((KV_HEADS,)),
            dma((KV_HEADS, 2)),
            dma((KV_HEADS, 8)),
            dma((KV_HEADS, 8)),
            dma((KV_HEADS, 8)),
            dma((KV_HEADS, 10)),
            dma((KV_HEADS, 9)),
            dma((KV_HEADS,)),
            dma((7,)),
            dma((7,)),
            dma((7,)),
            dma((3,)),
            dma((3,)),
            dma((7,)),
            dma((7,)),
            dma((7,)),
            dma((7,)),
        ],
        compiler_params=pltpu.CompilerParams(
            collective_id=0, has_side_effects=True, vmem_limit_bytes=56 * 2**20
        ),
        cost_estimate=pl.CostEstimate(flops=6 * 10**9, bytes_accessed=6 * 10**6, transcendentals=5 * 10**6),
        name="grads",
    )(
        queries[0], keys[0], values[0], prefix_keys, prefix_values, out_grad[0], boundaries, lengths, advantages
    )
    placed = pl.pallas_call(
        place_kernel,
        out_shape=shapes + [prefix_shape, prefix_shape],
        in_specs=[any_] * 3 + [vmem],
        out_specs=[any_] * 3 + [vmem] * 2,
        scratch_shapes=[
            pltpu.VMEM((ROWS, width), BF16),
            pltpu.VMEM((2, ROWS, kv_width), BF16),
            dma((6,)),
            dma((6,)),
        ],
        name="place",
    )(*outs)
    return placed[0][None], placed[1][None], placed[2][None], placed[3], placed[4]


def solution(mesh):
    in_specs = (
        P("dp", "ctx", None),
        P("dp", "ctx", None),
        P("dp", "ctx", None),
        P(),
        P(),
        P("dp", "ctx", None),
        P("dp", None),
        P("dp"),
        P("dp", None),
    )
    out_specs = (P("dp", "ctx", None), P("dp", "ctx", None), P("dp", "ctx", None), P(), P())
    return jax.shard_map(body, mesh=mesh, in_specs=in_specs, out_specs=out_specs, check_vma=False)
```

```python
import functools

import jax
import jax.numpy as jnp
from jax import lax
from jax.experimental import pallas as pl
from jax.experimental.pallas import tpu as pltpu
from jax.sharding import PartitionSpec as P

HEADS = 32
KV_HEADS = 8
GROUP = HEADS // KV_HEADS
HEAD_DIM = 128
PREFIX = 128
ROWS = 128
STEPS = 8
SCALE = HEAD_DIM**-0.5
SCALE_LOG2 = SCALE * 1.4426950408889634
NEG = -1e30
MESH = pl.DeviceIdType.MESH
F32 = jnp.float32
BF16 = jnp.bfloat16
AHEAD = 3
SECOND = 3
BACK = 5
LAG = 7
OVER = 4
WINDOW = 2
EARLY = 8
TAIL = 7
CONTRACT_LAST = (((1,), (1,)), ((), ()))
CONTRACT_FIRST = (((0,), (0,)), ((), ()))
CONTRACT_INNER = (((1,), (0,)), ((), ()))


def head_grads(h, ctx, keys_seen, unmasked, q_ref, og_ref, weight, kv, dkv, dq_ref, s_ref, d_ref):
    width = GROUP * HEAD_DIM
    cols = [pl.ds(pl.multiple_of(h * width + g * HEAD_DIM, HEAD_DIM), HEAD_DIM) for g in range(GROUP)]
    queries = jnp.concatenate([q_ref[:, c] for c in cols], axis=0)
    grads = jnp.concatenate(
        [(og_ref[:, c].astype(F32) * weight[...]).astype(BF16) for c in cols], axis=0
    )
    key_rows = kv[0, h, 0:keys_seen]
    value_rows = kv[1, h, 0:keys_seen]
    scores = lax.dot_general(key_rows, queries, CONTRACT_LAST, preferred_element_type=F32)
    query_pos = ctx * ROWS + lax.broadcasted_iota(jnp.int32, (1, ROWS), 1)
    query_pos = jnp.concatenate([query_pos] * GROUP, axis=1)
    key_pos = unmasked - PREFIX + lax.broadcasted_iota(jnp.int32, (keys_seen - unmasked, 1), 0)
    free, bound = scores[0:unmasked], scores[unmasked:]
    bound = jnp.where(key_pos <= query_pos, bound, NEG)
    s_ref[0:unmasked] = free
    s_ref[unmasked:keys_seen] = bound
    peak = jnp.maximum(
        jnp.max(free, axis=0, keepdims=True), jnp.max(bound, axis=0, keepdims=True)
    )
    d_ref[0:keys_seen] = lax.dot_general(value_rows, grads, CONTRACT_LAST, preferred_element_type=F32)
    raised = jnp.exp2((s_ref[0:keys_seen] - peak) * SCALE_LOG2)
    s_ref[0:keys_seen] = raised
    total = jnp.sum(raised, axis=0, keepdims=True)
    inverse = 1.0 / total
    delta = jnp.sum(raised * d_ref[0:keys_seen], axis=0, keepdims=True) * inverse
    probs = s_ref[0:keys_seen] * inverse
    score_grad = (probs * (d_ref[0:keys_seen] - delta)).astype(BF16)
    value_part = lax.dot_general(probs.astype(BF16), grads, CONTRACT_INNER, preferred_element_type=F32)
    dkv[1, h, 0:keys_seen] = value_part.astype(BF16)
    key_part = lax.dot_general(score_grad, queries, CONTRACT_INNER, preferred_element_type=F32)
    dkv[0, h, 0:keys_seen] = (key_part * SCALE).astype(BF16)
    query_part = lax.dot_general(key_rows, score_grad, CONTRACT_FIRST, preferred_element_type=F32)
    for g in range(GROUP):
        dq_ref[:, cols[g]] = (query_part[:, g * ROWS : (g + 1) * ROWS].T * SCALE).astype(BF16)


def kernel(
    q_hbm, k_hbm, v_hbm, pk_hbm, pv_hbm, og_hbm, bounds_ref, len_ref, adv_ref,
    dq_hbm, dk_hbm, dv_hbm, pg_hbm,
    q_ref, og_ref, dq_ref, dk_ref, dv_ref,
    kv, dkv, rb, s_ref, d_ref, weight,
    pbuf, acc, zbuf, ybuf, piece, fin, pgb,
    in_sem, kv_in_sem, out_sem, dq_sem, dkv_sem,
    kv_send, kv_recv, kv_recv_v, g_send, g_recv, p_send, p_recv,
    z_send, z_recv, y_send, y_recv, za_send, za_recv, f_send, f_recv,
):
    dp = lax.axis_index("dp")
    ctx = lax.axis_index("ctx")
    y = ctx % 4
    hi = ctx // 4
    z = hi * 4 + dp // 8
    own = dp % 8
    base = dp - own
    up = (y + 1) % 4
    down = (y + 3) % 4
    far = (y + 2) % 4

    def at_ctx(target):
        return (dp, target)

    def at_hi(target):
        return (dp, 4 + target)

    def at_own(target):
        return (base + target, ctx)

    def at_z(target):
        return ((target % 4) * 8 + own, (target // 4) * 4 + y)

    barrier = pltpu.get_barrier_semaphore()
    for step in range(1, 8):
        pl.semaphore_signal(barrier, inc=1, device_id=at_ctx((ctx + step) % 8), device_id_type=MESH)
        pl.semaphore_signal(barrier, inc=1, device_id=at_own((own + step) % 8), device_id_type=MESH)
        if step != 4:
            pl.semaphore_signal(barrier, inc=1, device_id=at_z((z + step) % 8), device_id_type=MESH)

    mine = pl.ds(pl.multiple_of((1 + ctx) * ROWS, ROWS), ROWS)
    kv_in = []
    for h in range(KV_HEADS):
        cols = pl.ds(h * HEAD_DIM, HEAD_DIM)
        pairs = (
            (k_hbm.at[:, cols], kv.at[0, h, mine]),
            (v_hbm.at[:, cols], kv.at[1, h, mine]),
            (pk_hbm.at[:, cols], kv.at[0, h, pl.ds(0, PREFIX)]),
            (pv_hbm.at[:, cols], kv.at[1, h, pl.ds(0, PREFIX)]),
        )
        for i, (s, d) in enumerate(pairs):
            kv_in.append(pltpu.make_async_copy(s, d, kv_in_sem.at[h, i]))
    for c in kv_in:
        c.start()
    big_in = [
        pltpu.make_async_copy(q_hbm, q_ref, in_sem.at[0]),
        pltpu.make_async_copy(og_hbm, og_ref, in_sem.at[1]),
    ]
    for c in big_in:
        c.start()

    def copy(src, dst, send, recv, target):
        return pltpu.make_async_remote_copy(
            src_ref=src, dst_ref=dst, send_sem=send, recv_sem=recv, device_id=target, device_id_type=MESH
        )

    def rows_of(j):
        return pl.ds(pl.multiple_of((1 + j) * ROWS, ROWS), ROWS)

    def block(ref, h, j):
        return ref.at[:, h, rows_of(j)]

    def half(ref, side, h, j):
        return ref.at[side, h, rows_of(j)]

    for j in range(1, 8):

        @pl.when(jnp.logical_and(ctx < j, hi == j // 4))
        def _(j=j):
            for h in range(KV_HEADS):
                kv[:, h, (1 + j) * ROWS : (2 + j) * ROWS] = jnp.zeros((2, ROWS, HEAD_DIM), BF16)

    pos = ctx * ROWS + lax.broadcasted_iota(jnp.int32, (ROWS, HEAD_DIM), 0)
    token = jnp.full((ROWS, HEAD_DIM), adv_ref[0, 0], F32)
    for s in range(1, STEPS):
        token = jnp.where(pos >= bounds_ref[0, s], adv_ref[0, s], token)
    weight[...] = jnp.where(pos < len_ref[0], token, 0.0)
    for c in kv_in:
        c.wait()
    for c in big_in:
        c.wait()

    pl.semaphore_wait(barrier, 20)

    def full_kv(kind, j, target):
        return lambda h: copy(block(kv, h, j), block(kv, h, j), kv_send.at[h, kind], kv_recv.at[h, j], target)

    def key_half(kind, j, target):
        return lambda h: copy(half(kv, 0, h, j), half(kv, 0, h, j), kv_send.at[h, kind], kv_recv.at[h, j], target)

    def value_half(kind, j, target):
        return lambda h: copy(half(kv, 1, h, j), half(kv, 1, h, j), kv_send.at[h, kind], kv_recv_v.at[h, j], target)

    lo_own = [(y + d < 4, full_kv(d - 1, ctx, at_ctx((y + d) % 4))) for d in (1, 2, 3)]
    lo_cross = [(None, full_kv(3, ctx, at_hi(y)))]
    hi_own = [
        (y < 3, full_kv(0, ctx, at_hi(up))),
        (y == 0, full_kv(1, ctx, at_hi(3))),
    ]
    hi_near = [(None, full_kv(2, y, at_hi(up))), (None, full_kv(3, y, at_hi(down)))]
    hi_pass_down = [
        (jnp.logical_or(y == 0, y == 1), full_kv(4, down, at_hi(up))),
        (y == 3, key_half(4, down, at_hi(up))),
    ]
    hi_pass_up = [
        (y == 0, full_kv(5, up, at_hi(down))),
        (y == 1, value_half(5, up, at_hi(down))),
    ]
    hi_pass_own = [
        (y == 1, key_half(6, 4 + down, at_hi(up))),
        (y == 2, full_kv(6, 4 + down, at_hi(up))),
        (y == 3, value_half(7, 4 + up, at_hi(down))),
    ]
    hi_pass = hi_pass_down + hi_pass_up + hi_pass_own

    def full_term(kind, j, slot, sem, target):
        return lambda h: copy(block(dkv, h, j), rb.at[slot, :, h], g_send.at[h, kind], g_recv.at[h, sem], target)

    def half_term(kind, side, j, slot, sem, target):
        return lambda h: copy(
            half(dkv, side, h, j), rb.at[slot, side, h], g_send.at[h, kind], g_recv.at[h, sem], target
        )

    lo_terms = [
        (y + d >= 4, full_term(d - 1, (y + d) % 4, 4 - d, 4 - d, at_ctx((y + d) % 4))) for d in (1, 2, 3)
    ]
    hi_first = [
        (y == 0, half_term(0, 0, far, 4, 4, at_hi(up))),
        (y == 0, half_term(1, 1, far, 4, 5, at_hi(down))),
        (y == 1, full_term(0, far, 4, 4, at_hi(down))),
        (y == 2, full_term(0, far, 6, 8, at_hi(down))),
        (y == 3, full_term(0, far, 5, 6, at_hi(up))),
        (y == 2, half_term(2, 0, 4 + far, 5, 6, at_hi(up))),
        (y == 2, half_term(3, 1, 4 + far, 5, 7, at_hi(down))),
        (y == 3, full_term(2, 4 + far, 4, 4, at_hi(down))),
        (y == 3, full_term(5, 4 + down, 2, 2, at_hi(down))),
    ]
    to_up = [(None, full_term(6, up, 0, 0, at_hi(up)))]
    to_down = [(None, full_term(7, down, 1, 1, at_hi(down)))]
    own_up = [(y == 3, full_term(8, 4 + up, 3, 3, at_hi(up)))]
    own_down = [(jnp.logical_or(y == 1, y == 2), full_term(5, 4 + down, 2, 2, at_hi(down)))]
    hi_second = to_up + to_down + own_up + own_down
    hi_back = [(None, full_term(9, y, 0, 0, at_ctx(y)))]

    def prefix_made(h):
        slot = jnp.minimum((own - h + 7) % 8, 6)
        return copy(dkv.at[:, h, pl.ds(0, PREFIX)], pbuf.at[slot], p_send.at[h], p_recv.at[slot], at_own(h))

    def start(entries, h):
        for cond, make in entries:
            if cond is None:
                make(h).start()
            else:
                pl.when(cond)(lambda make=make: make(h).start())

    def wait_send(entries, h):
        for cond, make in entries:
            if cond is None:
                make(h).wait_send()
            else:
                pl.when(cond)(lambda make=make: make(h).wait_send())

    def kv_arrived(h, j):
        copy(block(kv, h, j), block(kv, h, j), kv_send.at[h, 0], kv_recv.at[h, j], at_ctx(ctx)).wait_recv()

    def halves_arrived(h, j):
        copy(half(kv, 0, h, j), half(kv, 0, h, j), kv_send.at[h, 0], kv_recv.at[h, j], at_ctx(ctx)).wait_recv()
        copy(half(kv, 1, h, j), half(kv, 1, h, j), kv_send.at[h, 0], kv_recv_v.at[h, j], at_ctx(ctx)).wait_recv()

    def term_arrived(h, slot, sem=None):
        sem = slot if sem is None else sem
        copy(rb.at[slot, :, h], rb.at[slot, :, h], g_send.at[h, 0], g_recv.at[h, sem], at_ctx(ctx)).wait_recv()

    def half_term_arrived(h, slot, side, sem):
        copy(
            rb.at[slot, side, h], rb.at[slot, side, h], g_send.at[h, 0], g_recv.at[h, sem], at_ctx(ctx)
        ).wait_recv()

    grads = functools.partial(
        head_grads, q_ref=q_ref, og_ref=og_ref, weight=weight, kv=kv, dkv=dkv, dq_ref=dq_ref, s_ref=s_ref, d_ref=d_ref
    )

    def dq_copy(h):
        cols = pl.ds(pl.multiple_of(h * GROUP * HEAD_DIM, HEAD_DIM), GROUP * HEAD_DIM)
        return pltpu.make_async_copy(dq_ref.at[:, cols], dq_hbm.at[:, cols], dq_sem.at[h])

    def dkv_copies(h):
        cols = pl.ds(pl.multiple_of(h * HEAD_DIM, HEAD_DIM), HEAD_DIM)
        return (
            pltpu.make_async_copy(dk_ref.at[:, cols], dk_hbm.at[:, cols], dkv_sem.at[h, 0]),
            pltpu.make_async_copy(dv_ref.at[:, cols], dv_hbm.at[:, cols], dkv_sem.at[h, 1]),
        )

    def after_grads(h):
        pl.when(own != h)(lambda: prefix_made(h).start())
        dq_copy(h).start()

    def finish(h):
        def store(total):
            cols = pl.ds(pl.multiple_of(h * HEAD_DIM, HEAD_DIM), HEAD_DIM)
            dk_ref[:, cols] = total[0].astype(BF16)
            dv_ref[:, cols] = total[1].astype(BF16)
            for c in dkv_copies(h):
                c.start()

        @pl.when(hi == 0)
        def _():
            term_arrived(h, 0)
            for d in (1, 2, 3):

                @pl.when(y + d < 4)
                def _(d=d):
                    term_arrived(h, d)

                @pl.when(y + d >= 4)
                def _(d=d):
                    rb[d, :, h] = jnp.zeros((2, ROWS, HEAD_DIM), BF16)

            total = dkv[:, h, mine].astype(F32)
            for slot in range(4):
                total = total + rb[slot, :, h].astype(F32)
            store(total)

        @pl.when(hi == 1)
        def _():
            @pl.when(y < 3)
            def _():
                term_arrived(h, 2)

            @pl.when(y == 3)
            def _():
                rb[2, :, h] = jnp.zeros((2, ROWS, HEAD_DIM), BF16)

            @pl.when(y == 0)
            def _():
                term_arrived(h, 3)

            @pl.when(y > 0)
            def _():
                rb[3, :, h] = jnp.zeros((2, ROWS, HEAD_DIM), BF16)

            store(dkv[:, h, mine].astype(F32) + rb[2, :, h].astype(F32) + rb[3, :, h].astype(F32))

    def eighth(ref, i):
        return ref.at[pl.ds(pl.multiple_of(i * 32, 32), 32)]

    z_out = [
        lambda d=d: copy(eighth(acc, (z + d) % 8), zbuf.at[7 - d], z_send.at[d - 1], z_recv.at[7 - d], at_z((z + d) % 8))
        for d in range(1, 8)
    ]
    y_out = [
        lambda d=d: copy(ybuf.at[y], ybuf.at[y], y_send.at[d - 1], y_recv.at[3 - d], at_ctx(hi * 4 + (y + d) % 4))
        for d in range(1, 4)
    ]
    za_out = [
        lambda d=d: copy(piece, eighth(fin, z), za_send.at[d - 1], za_recv.at[7 - d], at_z((z + d) % 8))
        for d in range(1, 8)
    ]
    f_out = [
        lambda d=d: copy(pgb.at[own], pgb.at[own], f_send.at[d - 1], f_recv.at[7 - d], at_own((own + d) % 8))
        for d in range(1, 8)
    ]

    over = jnp.maximum(own + 1, OVER)

    def prefix_steps(t):
        @pl.when(t == over + 0)
        def _():
            for slot in range(7):
                copy(pbuf.at[slot], pbuf.at[slot], p_send.at[0], p_recv.at[slot], at_own(own)).wait_recv()
            total = dkv[:, own, 0:PREFIX].astype(F32)
            for slot in range(7):
                total = total + pbuf[slot].astype(F32)
            acc[...] = total.reshape(2 * PREFIX, HEAD_DIM)
            for c in z_out:
                c().start()

        @pl.when(t == over + 1)
        def _():
            for slot in range(7):
                copy(zbuf.at[slot], zbuf.at[slot], z_send.at[0], z_recv.at[slot], at_z(z)).wait_recv()
            total = acc[pl.ds(pl.multiple_of(z * 32, 32), 32)]
            for slot in range(7):
                total = total + zbuf[slot]
            ybuf[y] = total
            for c in y_out:
                c().start()

        @pl.when(t == over + 2)
        def _():
            for d in (1, 2, 3):
                there = (y + d) % 4
                copy(ybuf.at[there], ybuf.at[there], y_send.at[0], y_recv.at[d - 1], at_ctx(ctx)).wait_recv()
            total = ((ybuf[0] + ybuf[1]) + ybuf[2]) + ybuf[3]
            piece[...] = total
            fin[pl.ds(pl.multiple_of(z * 32, 32), 32)] = total
            for c in za_out:
                c().start()

        @pl.when(t == over + 3)
        def _():
            for d in range(1, 8):
                copy(piece, eighth(fin, (z + d) % 8), za_send.at[0], za_recv.at[d - 1], at_z(z)).wait_recv()
            pgb[own] = fin[...].astype(BF16)
            for c in f_out:
                c().start()

    def near(h):
        if EARLY == 0:
            start(hi_own, h)
        else:
            pl.when(h >= EARLY)(lambda: start(hi_own, h))
        kv_arrived(h, y)
        start(hi_near, h)

    def pass_on(h):
        kv_arrived(h, down)
        start(hi_pass_down, h)
        kv_arrived(h, up)
        start(hi_pass_up, h)
        pl.when(jnp.logical_or(y == 1, y == 2))(lambda: kv_arrived(h, 4 + down))
        pl.when(y == 3)(lambda: kv_arrived(h, 4))
        start(hi_pass_own, h)

    def all_here(h):
        pl.when(y == 0)(lambda: halves_arrived(h, far))
        pl.when(y > 0)(lambda: kv_arrived(h, far))
        pl.when(y == 2)(lambda: halves_arrived(h, 4))
        pl.when(y == 3)(lambda: kv_arrived(h, 5))
        pl.when(y == 3)(lambda: kv_arrived(h, 6))

    def add_half(side, h, j, slot, sem):
        half_term_arrived(h, slot, side, sem)
        rows = rows_of(j)
        dkv[side, h, rows] = (dkv[side, h, rows].astype(F32) + rb[slot, side, h].astype(F32)).astype(BF16)

    def add_full(h, j, slot, sem):
        term_arrived(h, slot, sem)
        rows = rows_of(j)
        dkv[:, h, rows] = (dkv[:, h, rows].astype(F32) + rb[slot, :, h].astype(F32)).astype(BF16)

    def first(h):
        start(hi_first, h)
        pl.when(y >= 2)(lambda: start(to_up, h))
        pl.when(y == 2)(lambda: start(to_down, h))

    def second(h):
        @pl.when(y == 0)
        def _():
            add_full(h, down, 4, 4)
            start(to_down, h)
            add_full(h, up, 5, 6)
            start(to_up, h)

        @pl.when(y == 1)
        def _():
            add_full(h, down, 6, 8)
            start(to_down, h)
            add_half(0, h, up, 4, 4)
            start(to_up, h)
            add_half(1, h, 4 + down, 5, 7)
            start(own_down, h)

        @pl.when(y == 2)
        def _():
            add_full(h, 4 + down, 4, 4)
            start(own_down, h)

        @pl.when(y == 3)
        def _():
            add_half(1, h, down, 4, 5)
            start(to_down, h)
            add_half(0, h, 4 + up, 5, 6)
            start(own_up, h)

    def back(h):
        term_arrived(h, 0)
        term_arrived(h, 1)
        rows = rows_of(y)
        total = dkv[:, h, rows].astype(F32) + rb[0, :, h].astype(F32) + rb[1, :, h].astype(F32)
        dkv[:, h, rows] = total.astype(BF16)
        start(hi_back, h)

    @pl.when(hi == 0)
    def _():
        for h in range(WINDOW):
            start(lo_cross, h)
        for h in range(KV_HEADS):
            start(lo_own, h)
        for h in range(WINDOW, KV_HEADS):
            wait_send(lo_cross, h - WINDOW)
            start(lo_cross, h)

    @pl.when(hi == 1)
    def _():
        for h in range(EARLY):
            start(hi_own, h)
        for h in range(AHEAD):
            near(h)
        for h in range(AHEAD - 1):
            pass_on(h)

    def step(t, c):
        @pl.when(jnp.logical_and(hi == 0, t < KV_HEADS))
        def _():
            for j in range(3):
                pl.when(j < ctx)(lambda j=j: kv_arrived(t, j))
            grads(t, ctx, 5 * ROWS, PREFIX)
            after_grads(t)
            start(lo_terms, t)

        @pl.when(hi == 1)
        def _():
            pl.when(t + AHEAD < KV_HEADS)(lambda: near(t + AHEAD))
            pl.when(t + AHEAD - 1 < KV_HEADS)(lambda: pass_on(t + AHEAD - 1))

            @pl.when(t < KV_HEADS)
            def _():
                all_here(t)
                grads(t, ctx, 9 * ROWS, 5 * ROWS)
                after_grads(t)
                first(t)

            pl.when(jnp.logical_and(t >= SECOND, t - SECOND < KV_HEADS))(lambda: second(t - SECOND))
            pl.when(jnp.logical_and(t >= BACK, t - BACK < KV_HEADS))(lambda: back(t - BACK))

        prefix_steps(t)
        pl.when(jnp.logical_and(t >= LAG, t - LAG < KV_HEADS))(lambda: finish(t - LAG))
        return c

    lax.fori_loop(0, KV_HEADS + TAIL, step, 0)

    for d in range(1, 8):
        there = (own + d) % 8
        copy(pgb.at[there], pgb.at[there], f_send.at[0], f_recv.at[d - 1], at_own(own)).wait_recv()
    out = pltpu.make_async_copy(pgb, pg_hbm, out_sem.at[0])
    out.start()

    for c in z_out + y_out + za_out + f_out:
        c().wait_send()

    def drain(h, c):
        pl.when(own != h)(lambda: prefix_made(h).wait_send())

        @pl.when(hi == 0)
        def _():
            wait_send(lo_own + lo_terms, h)
            pl.when(h >= KV_HEADS - WINDOW)(lambda: wait_send(lo_cross, h))

        @pl.when(hi == 1)
        def _():
            wait_send(hi_own + hi_near + hi_pass + hi_first + hi_second + hi_back, h)

        dq_copy(h).wait()
        for made in dkv_copies(h):
            made.wait()
        return c

    lax.fori_loop(0, KV_HEADS, drain, 0)
    out.wait()


def place_kernel(
    dq_in, dk_in, dv_in, pg_in, dq_out, dk_out, dv_out, dpk_out, dpv_out,
    big, small, prefix, wide, in_sem, out_sem, prefix_in, prefix_out,
):
    fetch = pltpu.make_async_copy(pg_in, prefix, prefix_in.at[0])
    fetch.start()
    parts = []
    for i in range(2):
        rows = pl.ds(i * 64, 64)
        parts.append((dq_in.at[rows], big.at[rows], dq_out.at[rows]))
    parts.append((dk_in, small.at[0], dk_out))
    parts.append((dv_in, small.at[1], dv_out))
    loads = [pltpu.make_async_copy(s, m, in_sem.at[i]) for i, (s, m, d) in enumerate(parts)]
    stores = [pltpu.make_async_copy(m, d, out_sem.at[i]) for i, (s, m, d) in enumerate(parts)]
    for c in loads:
        c.start()
    fetch.wait()
    for h in range(KV_HEADS):
        cols = slice(h * HEAD_DIM, (h + 1) * HEAD_DIM)
        wide[0, :, cols] = prefix[h, 0:PREFIX].astype(F32)
        wide[1, :, cols] = prefix[h, PREFIX:].astype(F32)
    puts = [
        pltpu.make_async_copy(wide.at[0], dpk_out, prefix_out.at[0]),
        pltpu.make_async_copy(wide.at[1], dpv_out, prefix_out.at[1]),
    ]
    for c in puts:
        c.start()
    for load, store in zip(loads, stores):
        load.wait()
        store.start()
    for c in puts + stores:
        c.wait()


def body(queries, keys, values, prefix_keys, prefix_values, out_grad, boundaries, lengths, advantages):
    width, kv_width = queries.shape[2], keys.shape[2]
    smem = pl.BlockSpec(memory_space=pltpu.SMEM)
    any_ = pl.BlockSpec(memory_space=pl.ANY)
    dma = pltpu.SemaphoreType.DMA
    key_rows = PREFIX + 8 * ROWS
    pair = (2, KV_HEADS, key_rows, HEAD_DIM)
    shapes = [
        jax.ShapeDtypeStruct((ROWS, width), BF16),
        jax.ShapeDtypeStruct((ROWS, kv_width), BF16),
        jax.ShapeDtypeStruct((ROWS, kv_width), BF16),
    ]
    prefix_shape = jax.ShapeDtypeStruct((PREFIX, kv_width), F32)
    outs = pl.pallas_call(
        kernel,
        out_shape=shapes + [jax.ShapeDtypeStruct((KV_HEADS, 2 * PREFIX, HEAD_DIM), BF16)],
        in_specs=[any_] * 6 + [smem] * 3,
        out_specs=[any_] * 4,
        scratch_shapes=[
            pltpu.VMEM((ROWS, width), BF16),
            pltpu.VMEM((ROWS, width), BF16),
            pltpu.VMEM((ROWS, width), BF16),
            pltpu.VMEM((ROWS, kv_width), BF16),
            pltpu.VMEM((ROWS, kv_width), BF16),
            pltpu.VMEM(pair, BF16),
            pltpu.VMEM(pair, BF16),
            pltpu.VMEM((7, 2, KV_HEADS, ROWS, HEAD_DIM), BF16),
            pltpu.VMEM((key_rows, GROUP * ROWS), F32),
            pltpu.VMEM((key_rows, GROUP * ROWS), F32),
            pltpu.VMEM((ROWS, HEAD_DIM), F32),
            pltpu.VMEM((7, 2, PREFIX, HEAD_DIM), BF16),
            pltpu.VMEM((2 * PREFIX, HEAD_DIM), F32),
            pltpu.VMEM((7, 32, HEAD_DIM), F32),
            pltpu.VMEM((4, 32, HEAD_DIM), F32),
            pltpu.VMEM((32, HEAD_DIM), F32),
            pltpu.VMEM((2 * PREFIX, HEAD_DIM), F32),
            pltpu.VMEM((KV_HEADS, 2 * PREFIX, HEAD_DIM), BF16),
            dma((2,)),
            dma((KV_HEADS, 4)),
            dma((1,)),
            dma((KV_HEADS,)),
            dma((KV_HEADS, 2)),
            dma((KV_HEADS, 8)),
            dma((KV_HEADS, 8)),
            dma((KV_HEADS, 8)),
            dma((KV_HEADS, 10)),
            dma((KV_HEADS, 9)),
            dma((KV_HEADS,)),
            dma((7,)),
            dma((7,)),
            dma((7,)),
            dma((3,)),
            dma((3,)),
            dma((7,)),
            dma((7,)),
            dma((7,)),
            dma((7,)),
        ],
        compiler_params=pltpu.CompilerParams(
            collective_id=0, has_side_effects=True, vmem_limit_bytes=56 * 2**20
        ),
        cost_estimate=pl.CostEstimate(flops=6 * 10**9, bytes_accessed=6 * 10**6, transcendentals=5 * 10**6),
        name="grads",
    )(
        queries[0], keys[0], values[0], prefix_keys, prefix_values, out_grad[0], boundaries, lengths, advantages
    )
    placed = pl.pallas_call(
        place_kernel,
        out_shape=shapes + [prefix_shape, prefix_shape],
        in_specs=[any_] * 4,
        out_specs=[any_] * 5,
        scratch_shapes=[
            pltpu.VMEM((ROWS, width), BF16),
            pltpu.VMEM((2, ROWS, kv_width), BF16),
            pltpu.VMEM((KV_HEADS, 2 * PREFIX, HEAD_DIM), BF16),
            pltpu.VMEM((2, PREFIX, kv_width), F32),
            dma((4,)),
            dma((4,)),
            dma((1,)),
            dma((2,)),
        ],
        name="place",
    )(*outs)
    return placed[0][None], placed[1][None], placed[2][None], placed[3], placed[4]


def solution(mesh):
    in_specs = (
        P("dp", "ctx", None),
        P("dp", "ctx", None),
        P("dp", "ctx", None),
        P(),
        P(),
        P("dp", "ctx", None),
        P("dp", None),
        P("dp"),
        P("dp", None),
    )
    out_specs = (P("dp", "ctx", None), P("dp", "ctx", None), P("dp", "ctx", None), P(), P())
    return jax.shard_map(body, mesh=mesh, in_specs=in_specs, out_specs=out_specs, check_vma=False)
```

```python
import functools

import jax
import jax.numpy as jnp
from jax import lax
from jax.experimental import pallas as pl
from jax.experimental.pallas import tpu as pltpu
from jax.sharding import PartitionSpec as P

HEADS = 32
KV_HEADS = 8
GROUP = HEADS // KV_HEADS
HEAD_DIM = 128
PREFIX = 128
ROWS = 128
STEPS = 8
SCALE = HEAD_DIM**-0.5
SCALE_LOG2 = SCALE * 1.4426950408889634
NEG = -1e30
MESH = pl.DeviceIdType.MESH
F32 = jnp.float32
BF16 = jnp.bfloat16
AHEAD = 3
SECOND = 3
BACK = 5
LAG = 7
OVER = 5
WINDOW = 1
EARLY = 8
TAIL = 7
CONTRACT_LAST = (((1,), (1,)), ((), ()))
CONTRACT_FIRST = (((0,), (0,)), ((), ()))
CONTRACT_INNER = (((1,), (0,)), ((), ()))


def head_grads(h, ctx, keys_seen, unmasked, q_ref, og_ref, weight, kv, dkv, dq_ref, s_ref, d_ref):
    width = GROUP * HEAD_DIM
    cols = [pl.ds(pl.multiple_of(h * width + g * HEAD_DIM, HEAD_DIM), HEAD_DIM) for g in range(GROUP)]
    queries = jnp.concatenate([q_ref[:, c] for c in cols], axis=0)
    grads = jnp.concatenate(
        [(og_ref[:, c].astype(F32) * weight[...]).astype(BF16) for c in cols], axis=0
    )
    key_rows = kv[0, h, 0:keys_seen]
    value_rows = kv[1, h, 0:keys_seen]
    scores = lax.dot_general(key_rows, queries, CONTRACT_LAST, preferred_element_type=F32)
    query_pos = ctx * ROWS + lax.broadcasted_iota(jnp.int32, (1, ROWS), 1)
    query_pos = jnp.concatenate([query_pos] * GROUP, axis=1)
    key_pos = unmasked - PREFIX + lax.broadcasted_iota(jnp.int32, (keys_seen - unmasked, 1), 0)
    free, bound = scores[0:unmasked], scores[unmasked:]
    bound = jnp.where(key_pos <= query_pos, bound, NEG)
    s_ref[0:unmasked] = free
    s_ref[unmasked:keys_seen] = bound
    peak = jnp.maximum(
        jnp.max(free, axis=0, keepdims=True), jnp.max(bound, axis=0, keepdims=True)
    )
    d_ref[0:keys_seen] = lax.dot_general(value_rows, grads, CONTRACT_LAST, preferred_element_type=F32)
    raised = jnp.exp2((s_ref[0:keys_seen] - peak) * SCALE_LOG2)
    s_ref[0:keys_seen] = raised
    total = jnp.sum(raised, axis=0, keepdims=True)
    inverse = 1.0 / total
    delta = jnp.sum(raised * d_ref[0:keys_seen], axis=0, keepdims=True) * inverse
    probs = s_ref[0:keys_seen] * inverse
    score_grad = (probs * (d_ref[0:keys_seen] - delta)).astype(BF16)
    value_part = lax.dot_general(probs.astype(BF16), grads, CONTRACT_INNER, preferred_element_type=F32)
    dkv[1, h, 0:keys_seen] = value_part.astype(BF16)
    key_part = lax.dot_general(score_grad, queries, CONTRACT_INNER, preferred_element_type=F32)
    dkv[0, h, 0:keys_seen] = (key_part * SCALE).astype(BF16)
    query_part = lax.dot_general(key_rows, score_grad, CONTRACT_FIRST, preferred_element_type=F32)
    for g in range(GROUP):
        dq_ref[:, cols[g]] = (query_part[:, g * ROWS : (g + 1) * ROWS].T * SCALE).astype(BF16)


def kernel(
    q_hbm, k_hbm, v_hbm, pk_hbm, pv_hbm, og_hbm, bounds_ref, len_ref, adv_ref,
    dq_hbm, dk_hbm, dv_hbm, pg_hbm,
    q_ref, og_ref, dq_ref, dk_ref, dv_ref,
    kv, dkv, rb, s_ref, d_ref, weight,
    pbuf, acc, zbuf, ybuf, piece, fin, pgb,
    in_sem, kv_in_sem, out_sem, dq_sem, dkv_sem,
    kv_send, kv_recv, kv_recv_v, g_send, g_recv, p_send, p_recv,
    z_send, z_recv, y_send, y_recv, za_send, za_recv, f_send, f_recv,
):
    dp = lax.axis_index("dp")
    ctx = lax.axis_index("ctx")
    y = ctx % 4
    hi = ctx // 4
    z = hi * 4 + dp // 8
    own = dp % 8
    base = dp - own
    up = (y + 1) % 4
    down = (y + 3) % 4
    far = (y + 2) % 4

    def at_ctx(target):
        return (dp, target)

    def at_hi(target):
        return (dp, 4 + target)

    def at_own(target):
        return (base + target, ctx)

    def at_z(target):
        return ((target % 4) * 8 + own, (target // 4) * 4 + y)

    barrier = pltpu.get_barrier_semaphore()
    for step in range(1, 8):
        pl.semaphore_signal(barrier, inc=1, device_id=at_ctx((ctx + step) % 8), device_id_type=MESH)
        pl.semaphore_signal(barrier, inc=1, device_id=at_own((own + step) % 8), device_id_type=MESH)
        if step != 4:
            pl.semaphore_signal(barrier, inc=1, device_id=at_z((z + step) % 8), device_id_type=MESH)

    mine = pl.ds(pl.multiple_of((1 + ctx) * ROWS, ROWS), ROWS)
    kv_in = []
    for h in range(KV_HEADS):
        cols = pl.ds(h * HEAD_DIM, HEAD_DIM)
        pairs = (
            (k_hbm.at[:, cols], kv.at[0, h, mine]),
            (v_hbm.at[:, cols], kv.at[1, h, mine]),
            (pk_hbm.at[:, cols], kv.at[0, h, pl.ds(0, PREFIX)]),
            (pv_hbm.at[:, cols], kv.at[1, h, pl.ds(0, PREFIX)]),
        )
        for i, (s, d) in enumerate(pairs):
            kv_in.append(pltpu.make_async_copy(s, d, kv_in_sem.at[h, i]))
    for c in kv_in:
        c.start()
    big_in = [
        pltpu.make_async_copy(q_hbm, q_ref, in_sem.at[0]),
        pltpu.make_async_copy(og_hbm, og_ref, in_sem.at[1]),
    ]
    for c in big_in:
        c.start()

    def copy(src, dst, send, recv, target):
        return pltpu.make_async_remote_copy(
            src_ref=src, dst_ref=dst, send_sem=send, recv_sem=recv, device_id=target, device_id_type=MESH
        )

    def rows_of(j):
        return pl.ds(pl.multiple_of((1 + j) * ROWS, ROWS), ROWS)

    def block(ref, h, j):
        return ref.at[:, h, rows_of(j)]

    def half(ref, side, h, j):
        return ref.at[side, h, rows_of(j)]

    for j in range(1, 8):

        @pl.when(jnp.logical_and(ctx < j, hi == j // 4))
        def _(j=j):
            for h in range(KV_HEADS):
                kv[:, h, (1 + j) * ROWS : (2 + j) * ROWS] = jnp.zeros((2, ROWS, HEAD_DIM), BF16)

    pos = ctx * ROWS + lax.broadcasted_iota(jnp.int32, (ROWS, HEAD_DIM), 0)
    token = jnp.full((ROWS, HEAD_DIM), adv_ref[0, 0], F32)
    for s in range(1, STEPS):
        token = jnp.where(pos >= bounds_ref[0, s], adv_ref[0, s], token)
    weight[...] = jnp.where(pos < len_ref[0], token, 0.0)
    for c in kv_in:
        c.wait()
    for c in big_in:
        c.wait()

    pl.semaphore_wait(barrier, 20)

    def full_kv(kind, j, target):
        return lambda h: copy(block(kv, h, j), block(kv, h, j), kv_send.at[h, kind], kv_recv.at[h, j], target)

    def key_half(kind, j, target):
        return lambda h: copy(half(kv, 0, h, j), half(kv, 0, h, j), kv_send.at[h, kind], kv_recv.at[h, j], target)

    def value_half(kind, j, target):
        return lambda h: copy(half(kv, 1, h, j), half(kv, 1, h, j), kv_send.at[h, kind], kv_recv_v.at[h, j], target)

    lo_own = [(y + d < 4, full_kv(d - 1, ctx, at_ctx((y + d) % 4))) for d in (1, 2, 3)]
    lo_cross = [(None, full_kv(3, ctx, at_hi(y)))]
    hi_own = [
        (y < 3, full_kv(0, ctx, at_hi(up))),
        (y == 0, full_kv(1, ctx, at_hi(3))),
    ]
    hi_near = [(None, full_kv(2, y, at_hi(up))), (None, full_kv(3, y, at_hi(down)))]
    hi_pass_down = [
        (jnp.logical_or(y == 0, y == 1), full_kv(4, down, at_hi(up))),
        (y == 3, key_half(4, down, at_hi(up))),
    ]
    hi_pass_up = [
        (y == 0, full_kv(5, up, at_hi(down))),
        (y == 1, value_half(5, up, at_hi(down))),
    ]
    hi_pass_own = [
        (y == 1, key_half(6, 4 + down, at_hi(up))),
        (y == 2, full_kv(6, 4 + down, at_hi(up))),
        (y == 3, value_half(7, 4 + up, at_hi(down))),
    ]
    hi_pass = hi_pass_down + hi_pass_up + hi_pass_own

    def full_term(kind, j, slot, sem, target):
        return lambda h: copy(block(dkv, h, j), rb.at[slot, :, h], g_send.at[h, kind], g_recv.at[h, sem], target)

    def half_term(kind, side, j, slot, sem, target):
        return lambda h: copy(
            half(dkv, side, h, j), rb.at[slot, side, h], g_send.at[h, kind], g_recv.at[h, sem], target
        )

    lo_terms = [
        (y + d >= 4, full_term(d - 1, (y + d) % 4, 4 - d, 4 - d, at_ctx((y + d) % 4))) for d in (1, 2, 3)
    ]
    hi_first = [
        (y == 0, half_term(0, 0, far, 4, 4, at_hi(up))),
        (y == 0, half_term(1, 1, far, 4, 5, at_hi(down))),
        (y == 1, full_term(0, far, 4, 4, at_hi(down))),
        (y == 2, full_term(0, far, 6, 8, at_hi(down))),
        (y == 3, full_term(0, far, 5, 6, at_hi(up))),
        (y == 2, half_term(2, 0, 4 + far, 5, 6, at_hi(up))),
        (y == 2, half_term(3, 1, 4 + far, 5, 7, at_hi(down))),
        (y == 3, full_term(2, 4 + far, 4, 4, at_hi(down))),
        (y == 3, full_term(5, 4 + down, 2, 2, at_hi(down))),
    ]
    to_up = [(None, full_term(6, up, 0, 0, at_hi(up)))]
    to_down = [(None, full_term(7, down, 1, 1, at_hi(down)))]
    own_up = [(y == 3, full_term(8, 4 + up, 3, 3, at_hi(up)))]
    own_down = [(jnp.logical_or(y == 1, y == 2), full_term(5, 4 + down, 2, 2, at_hi(down)))]
    hi_second = to_up + to_down + own_up + own_down
    hi_back = [(None, full_term(9, y, 0, 0, at_ctx(y)))]

    def prefix_made(h):
        slot = jnp.minimum((own - h + 7) % 8, 6)
        return copy(dkv.at[:, h, pl.ds(0, PREFIX)], pbuf.at[slot], p_send.at[h], p_recv.at[slot], at_own(h))

    def start(entries, h):
        for cond, make in entries:
            if cond is None:
                make(h).start()
            else:
                pl.when(cond)(lambda make=make: make(h).start())

    def wait_send(entries, h):
        for cond, make in entries:
            if cond is None:
                make(h).wait_send()
            else:
                pl.when(cond)(lambda make=make: make(h).wait_send())

    def kv_arrived(h, j):
        copy(block(kv, h, j), block(kv, h, j), kv_send.at[h, 0], kv_recv.at[h, j], at_ctx(ctx)).wait_recv()

    def halves_arrived(h, j):
        copy(half(kv, 0, h, j), half(kv, 0, h, j), kv_send.at[h, 0], kv_recv.at[h, j], at_ctx(ctx)).wait_recv()
        copy(half(kv, 1, h, j), half(kv, 1, h, j), kv_send.at[h, 0], kv_recv_v.at[h, j], at_ctx(ctx)).wait_recv()

    def term_arrived(h, slot, sem=None):
        sem = slot if sem is None else sem
        copy(rb.at[slot, :, h], rb.at[slot, :, h], g_send.at[h, 0], g_recv.at[h, sem], at_ctx(ctx)).wait_recv()

    def half_term_arrived(h, slot, side, sem):
        copy(
            rb.at[slot, side, h], rb.at[slot, side, h], g_send.at[h, 0], g_recv.at[h, sem], at_ctx(ctx)
        ).wait_recv()

    grads = functools.partial(
        head_grads, q_ref=q_ref, og_ref=og_ref, weight=weight, kv=kv, dkv=dkv, dq_ref=dq_ref, s_ref=s_ref, d_ref=d_ref
    )

    def dq_copy(h):
        cols = pl.ds(pl.multiple_of(h * GROUP * HEAD_DIM, HEAD_DIM), GROUP * HEAD_DIM)
        return pltpu.make_async_copy(dq_ref.at[:, cols], dq_hbm.at[:, cols], dq_sem.at[h])

    def dkv_copies(h):
        cols = pl.ds(pl.multiple_of(h * HEAD_DIM, HEAD_DIM), HEAD_DIM)
        return (
            pltpu.make_async_copy(dk_ref.at[:, cols], dk_hbm.at[:, cols], dkv_sem.at[h, 0]),
            pltpu.make_async_copy(dv_ref.at[:, cols], dv_hbm.at[:, cols], dkv_sem.at[h, 1]),
        )

    def after_grads(h):
        pl.when(own != h)(lambda: prefix_made(h).start())
        dq_copy(h).start()

    def finish(h):
        def store(total):
            cols = pl.ds(pl.multiple_of(h * HEAD_DIM, HEAD_DIM), HEAD_DIM)
            dk_ref[:, cols] = total[0].astype(BF16)
            dv_ref[:, cols] = total[1].astype(BF16)
            for c in dkv_copies(h):
                c.start()

        @pl.when(hi == 0)
        def _():
            term_arrived(h, 0)
            for d in (1, 2, 3):

                @pl.when(y + d < 4)
                def _(d=d):
                    term_arrived(h, d)

                @pl.when(y + d >= 4)
                def _(d=d):
                    rb[d, :, h] = jnp.zeros((2, ROWS, HEAD_DIM), BF16)

            total = dkv[:, h, mine].astype(F32)
            for slot in range(4):
                total = total + rb[slot, :, h].astype(F32)
            store(total)

        @pl.when(hi == 1)
        def _():
            @pl.when(y < 3)
            def _():
                term_arrived(h, 2)

            @pl.when(y == 3)
            def _():
                rb[2, :, h] = jnp.zeros((2, ROWS, HEAD_DIM), BF16)

            @pl.when(y == 0)
            def _():
                term_arrived(h, 3)

            @pl.when(y > 0)
            def _():
                rb[3, :, h] = jnp.zeros((2, ROWS, HEAD_DIM), BF16)

            store(dkv[:, h, mine].astype(F32) + rb[2, :, h].astype(F32) + rb[3, :, h].astype(F32))

    def eighth(ref, i):
        return ref.at[pl.ds(pl.multiple_of(i * 32, 32), 32)]

    z_out = [
        lambda d=d: copy(eighth(acc, (z + d) % 8), zbuf.at[7 - d], z_send.at[d - 1], z_recv.at[7 - d], at_z((z + d) % 8))
        for d in range(1, 8)
    ]
    y_out = [
        lambda d=d: copy(ybuf.at[y], ybuf.at[y], y_send.at[d - 1], y_recv.at[3 - d], at_ctx(hi * 4 + (y + d) % 4))
        for d in range(1, 4)
    ]
    za_out = [
        lambda d=d: copy(piece, eighth(fin, z), za_send.at[d - 1], za_recv.at[7 - d], at_z((z + d) % 8))
        for d in range(1, 8)
    ]
    f_out = [
        lambda d=d: copy(pgb.at[own], pgb.at[own], f_send.at[d - 1], f_recv.at[7 - d], at_own((own + d) % 8))
        for d in range(1, 8)
    ]

    over = jnp.maximum(own + 1, OVER)

    def prefix_steps(t):
        @pl.when(t == over + 0)
        def _():
            for slot in range(7):
                copy(pbuf.at[slot], pbuf.at[slot], p_send.at[0], p_recv.at[slot], at_own(own)).wait_recv()
            total = dkv[:, own, 0:PREFIX].astype(F32)
            for slot in range(7):
                total = total + pbuf[slot].astype(F32)
            acc[...] = total.reshape(2 * PREFIX, HEAD_DIM)
            for c in z_out:
                c().start()

        @pl.when(t == over + 1)
        def _():
            for slot in range(7):
                copy(zbuf.at[slot], zbuf.at[slot], z_send.at[0], z_recv.at[slot], at_z(z)).wait_recv()
            total = acc[pl.ds(pl.multiple_of(z * 32, 32), 32)]
            for slot in range(7):
                total = total + zbuf[slot]
            ybuf[y] = total
            for c in y_out:
                c().start()

        @pl.when(t == over + 2)
        def _():
            for d in (1, 2, 3):
                there = (y + d) % 4
                copy(ybuf.at[there], ybuf.at[there], y_send.at[0], y_recv.at[d - 1], at_ctx(ctx)).wait_recv()
            total = ((ybuf[0] + ybuf[1]) + ybuf[2]) + ybuf[3]
            piece[...] = total
            fin[pl.ds(pl.multiple_of(z * 32, 32), 32)] = total
            for c in za_out:
                c().start()

        @pl.when(t == over + 3)
        def _():
            for d in range(1, 8):
                copy(piece, eighth(fin, (z + d) % 8), za_send.at[0], za_recv.at[d - 1], at_z(z)).wait_recv()
            pgb[own] = fin[...].astype(BF16)
            for c in f_out:
                c().start()

    def near(h):
        if EARLY == 0:
            start(hi_own, h)
        else:
            pl.when(h >= EARLY)(lambda: start(hi_own, h))
        kv_arrived(h, y)
        start(hi_near, h)

    def pass_on(h):
        kv_arrived(h, down)
        start(hi_pass_down, h)
        kv_arrived(h, up)
        start(hi_pass_up, h)
        pl.when(jnp.logical_or(y == 1, y == 2))(lambda: kv_arrived(h, 4 + down))
        pl.when(y == 3)(lambda: kv_arrived(h, 4))
        start(hi_pass_own, h)

    def all_here(h):
        pl.when(y == 0)(lambda: halves_arrived(h, far))
        pl.when(y > 0)(lambda: kv_arrived(h, far))
        pl.when(y == 2)(lambda: halves_arrived(h, 4))
        pl.when(y == 3)(lambda: kv_arrived(h, 5))
        pl.when(y == 3)(lambda: kv_arrived(h, 6))

    def add_half(side, h, j, slot, sem):
        half_term_arrived(h, slot, side, sem)
        rows = rows_of(j)
        dkv[side, h, rows] = (dkv[side, h, rows].astype(F32) + rb[slot, side, h].astype(F32)).astype(BF16)

    def add_full(h, j, slot, sem):
        term_arrived(h, slot, sem)
        rows = rows_of(j)
        dkv[:, h, rows] = (dkv[:, h, rows].astype(F32) + rb[slot, :, h].astype(F32)).astype(BF16)

    def first(h):
        start(hi_first, h)
        pl.when(y >= 2)(lambda: start(to_up, h))
        pl.when(y == 2)(lambda: start(to_down, h))

    def second(h):
        @pl.when(y == 0)
        def _():
            add_full(h, down, 4, 4)
            start(to_down, h)
            add_full(h, up, 5, 6)
            start(to_up, h)

        @pl.when(y == 1)
        def _():
            add_full(h, down, 6, 8)
            start(to_down, h)
            add_half(0, h, up, 4, 4)
            start(to_up, h)
            add_half(1, h, 4 + down, 5, 7)
            start(own_down, h)

        @pl.when(y == 2)
        def _():
            add_full(h, 4 + down, 4, 4)
            start(own_down, h)

        @pl.when(y == 3)
        def _():
            add_half(1, h, down, 4, 5)
            start(to_down, h)
            add_half(0, h, 4 + up, 5, 6)
            start(own_up, h)

    def back(h):
        term_arrived(h, 0)
        term_arrived(h, 1)
        rows = rows_of(y)
        total = dkv[:, h, rows].astype(F32) + rb[0, :, h].astype(F32) + rb[1, :, h].astype(F32)
        dkv[:, h, rows] = total.astype(BF16)
        start(hi_back, h)

    @pl.when(hi == 0)
    def _():
        for h in range(WINDOW):
            start(lo_cross, h)
        for h in range(KV_HEADS):
            start(lo_own, h)
        for h in range(WINDOW, KV_HEADS):
            wait_send(lo_cross, h - WINDOW)
            start(lo_cross, h)

    @pl.when(hi == 1)
    def _():
        for h in range(EARLY):
            start(hi_own, h)
        for h in range(AHEAD):
            near(h)
        for h in range(AHEAD - 1):
            pass_on(h)

    def step(t, c):
        @pl.when(jnp.logical_and(hi == 0, t < KV_HEADS))
        def _():
            for j in range(3):
                pl.when(j < ctx)(lambda j=j: kv_arrived(t, j))
            grads(t, ctx, 5 * ROWS, PREFIX)
            after_grads(t)
            start(lo_terms, t)

        @pl.when(hi == 1)
        def _():
            pl.when(t + AHEAD < KV_HEADS)(lambda: near(t + AHEAD))
            pl.when(t + AHEAD - 1 < KV_HEADS)(lambda: pass_on(t + AHEAD - 1))

            pl.when(jnp.logical_and(t >= SECOND, t - SECOND < KV_HEADS))(lambda: second(t - SECOND))
            pl.when(jnp.logical_and(t >= BACK, t - BACK < KV_HEADS))(lambda: back(t - BACK))
            @pl.when(t < KV_HEADS)
            def _():
                all_here(t)
                grads(t, ctx, 9 * ROWS, 5 * ROWS)
                after_grads(t)
                first(t)


        prefix_steps(t)
        pl.when(jnp.logical_and(t >= LAG, t - LAG < KV_HEADS))(lambda: finish(t - LAG))
        return c

    lax.fori_loop(0, KV_HEADS + TAIL, step, 0)

    for d in range(1, 8):
        there = (own + d) % 8
        copy(pgb.at[there], pgb.at[there], f_send.at[0], f_recv.at[d - 1], at_own(own)).wait_recv()
    out = pltpu.make_async_copy(pgb, pg_hbm, out_sem.at[0])
    out.start()

    for c in z_out + y_out + za_out + f_out:
        c().wait_send()

    def drain(h, c):
        pl.when(own != h)(lambda: prefix_made(h).wait_send())

        @pl.when(hi == 0)
        def _():
            wait_send(lo_own + lo_terms, h)
            pl.when(h >= KV_HEADS - WINDOW)(lambda: wait_send(lo_cross, h))

        @pl.when(hi == 1)
        def _():
            wait_send(hi_own + hi_near + hi_pass + hi_first + hi_second + hi_back, h)

        dq_copy(h).wait()
        for made in dkv_copies(h):
            made.wait()
        return c

    lax.fori_loop(0, KV_HEADS, drain, 0)
    out.wait()


def place_kernel(
    dq_in, dk_in, dv_in, pg_in, dq_out, dk_out, dv_out, dpk_out, dpv_out,
    big, small, prefix, wide, in_sem, out_sem, prefix_in, prefix_out,
):
    fetch = pltpu.make_async_copy(pg_in, prefix, prefix_in.at[0])
    fetch.start()
    parts = []
    for i in range(2):
        rows = pl.ds(i * 64, 64)
        parts.append((dq_in.at[rows], big.at[rows], dq_out.at[rows]))
    parts.append((dk_in, small.at[0], dk_out))
    parts.append((dv_in, small.at[1], dv_out))
    loads = [pltpu.make_async_copy(s, m, in_sem.at[i]) for i, (s, m, d) in enumerate(parts)]
    stores = [pltpu.make_async_copy(m, d, out_sem.at[i]) for i, (s, m, d) in enumerate(parts)]
    for c in loads:
        c.start()
    fetch.wait()
    for h in range(KV_HEADS):
        cols = slice(h * HEAD_DIM, (h + 1) * HEAD_DIM)
        wide[0, :, cols] = prefix[h, 0:PREFIX].astype(F32)
        wide[1, :, cols] = prefix[h, PREFIX:].astype(F32)
    puts = [
        pltpu.make_async_copy(wide.at[0], dpk_out, prefix_out.at[0]),
        pltpu.make_async_copy(wide.at[1], dpv_out, prefix_out.at[1]),
    ]
    for c in puts:
        c.start()
    for load, store in zip(loads, stores):
        load.wait()
        store.start()
    for c in puts + stores:
        c.wait()


def body(queries, keys, values, prefix_keys, prefix_values, out_grad, boundaries, lengths, advantages):
    width, kv_width = queries.shape[2], keys.shape[2]
    smem = pl.BlockSpec(memory_space=pltpu.SMEM)
    any_ = pl.BlockSpec(memory_space=pl.ANY)
    dma = pltpu.SemaphoreType.DMA
    key_rows = PREFIX + 8 * ROWS
    pair = (2, KV_HEADS, key_rows, HEAD_DIM)
    shapes = [
        jax.ShapeDtypeStruct((ROWS, width), BF16),
        jax.ShapeDtypeStruct((ROWS, kv_width), BF16),
        jax.ShapeDtypeStruct((ROWS, kv_width), BF16),
    ]
    prefix_shape = jax.ShapeDtypeStruct((PREFIX, kv_width), F32)
    outs = pl.pallas_call(
        kernel,
        out_shape=shapes + [jax.ShapeDtypeStruct((KV_HEADS, 2 * PREFIX, HEAD_DIM), BF16)],
        in_specs=[any_] * 6 + [smem] * 3,
        out_specs=[any_] * 4,
        scratch_shapes=[
            pltpu.VMEM((ROWS, width), BF16),
            pltpu.VMEM((ROWS, width), BF16),
            pltpu.VMEM((ROWS, width), BF16),
            pltpu.VMEM((ROWS, kv_width), BF16),
            pltpu.VMEM((ROWS, kv_width), BF16),
            pltpu.VMEM(pair, BF16),
            pltpu.VMEM(pair, BF16),
            pltpu.VMEM((7, 2, KV_HEADS, ROWS, HEAD_DIM), BF16),
            pltpu.VMEM((key_rows, GROUP * ROWS), F32),
            pltpu.VMEM((key_rows, GROUP * ROWS), F32),
            pltpu.VMEM((ROWS, HEAD_DIM), F32),
            pltpu.VMEM((7, 2, PREFIX, HEAD_DIM), BF16),
            pltpu.VMEM((2 * PREFIX, HEAD_DIM), F32),
            pltpu.VMEM((7, 32, HEAD_DIM), F32),
            pltpu.VMEM((4, 32, HEAD_DIM), F32),
            pltpu.VMEM((32, HEAD_DIM), F32),
            pltpu.VMEM((2 * PREFIX, HEAD_DIM), F32),
            pltpu.VMEM((KV_HEADS, 2 * PREFIX, HEAD_DIM), BF16),
            dma((2,)),
            dma((KV_HEADS, 4)),
            dma((1,)),
            dma((KV_HEADS,)),
            dma((KV_HEADS, 2)),
            dma((KV_HEADS, 8)),
            dma((KV_HEADS, 8)),
            dma((KV_HEADS, 8)),
            dma((KV_HEADS, 10)),
            dma((KV_HEADS, 9)),
            dma((KV_HEADS,)),
            dma((7,)),
            dma((7,)),
            dma((7,)),
            dma((3,)),
            dma((3,)),
            dma((7,)),
            dma((7,)),
            dma((7,)),
            dma((7,)),
        ],
        compiler_params=pltpu.CompilerParams(
            collective_id=0, has_side_effects=True, vmem_limit_bytes=56 * 2**20
        ),
        cost_estimate=pl.CostEstimate(flops=6 * 10**9, bytes_accessed=6 * 10**6, transcendentals=5 * 10**6),
        name="grads",
    )(
        queries[0], keys[0], values[0], prefix_keys, prefix_values, out_grad[0], boundaries, lengths, advantages
    )
    placed = pl.pallas_call(
        place_kernel,
        out_shape=shapes + [prefix_shape, prefix_shape],
        in_specs=[any_] * 4,
        out_specs=[any_] * 5,
        scratch_shapes=[
            pltpu.VMEM((ROWS, width), BF16),
            pltpu.VMEM((2, ROWS, kv_width), BF16),
            pltpu.VMEM((KV_HEADS, 2 * PREFIX, HEAD_DIM), BF16),
            pltpu.VMEM((2, PREFIX, kv_width), F32),
            dma((4,)),
            dma((4,)),
            dma((1,)),
            dma((2,)),
        ],
        name="place",
    )(*outs)
    return placed[0][None], placed[1][None], placed[2][None], placed[3], placed[4]


def solution(mesh):
    in_specs = (
        P("dp", "ctx", None),
        P("dp", "ctx", None),
        P("dp", "ctx", None),
        P(),
        P(),
        P("dp", "ctx", None),
        P("dp", None),
        P("dp"),
        P("dp", None),
    )
    out_specs = (P("dp", "ctx", None), P("dp", "ctx", None), P("dp", "ctx", None), P(), P())
    return jax.shard_map(body, mesh=mesh, in_specs=in_specs, out_specs=out_specs, check_vma=False)
```
